256 devices in a mesh: seq: 64 (over y, z, x_lo), chan: 4 (over x_hi, core).
Axes of the slice: x: 4 (x_hi: 2, x_lo: 2; x = x_hi * 2 + x_lo), y: 4, z: 8, core: 2. Of those that a mesh axis runs over, the one named last changes fastest.
Arguments:
- inputs: bfloat16 [2, 65536, 2048], P(None, 'seq', 'chan'), may hold values from -6 to 6
- mix_first: bfloat16 [256, 256, 256], P('seq'), may hold values from -0.375 to 0.375
- mix_second: bfloat16 [256, 256, 256], P('seq'), may hold values from -0.375 to 0.375
- gate_scale: float32 [2048], P('chan'), may hold values from 0.5 to 2
- gate_bias: float32 [2048], P('chan'), may hold values from -3 to 3
- up_first: bfloat16 [4, 512, 512], P('chan'), may hold values from -0.25 to 0.25
- up_second: bfloat16 [4, 2048, 512], P('chan'), may hold values from -0.25 to 0.25
- down_first: bfloat16 [4, 512, 2048], P('chan'), may hold values from -0.125 to 0.125
- down_second: bfloat16 [4, 512, 512], P('chan'), may hold values from -0.25 to 0.25
Outputs:
- layer_out: bfloat16 [2, 65536, 2048], P(None, ('seq', 'chan'))
The draws below stay inside these ranges and needn't reach their ends.
All inputs are finite; a program needn't handle non-finite values.
Results may differ from the reference program's by a relative error of at most 0.008.
Values may be sent and summed in bfloat16 or wider, within the bound.
No kernel may reach another device: no remote copies, remote signals or barrier semaphores. Data moves between devices by JAX's collectives and lax.ppermute only.
A program may use at most 128 MiB of HBM per device.

```python
import math
import jax
import jax.numpy as jnp
from jax import lax

D = 2048
BLK = 256
SEQS = 2
NC = 4
NA = 256
LEN = 65536
CB = 512
HB = 2048


def block_scale(key, shape, split, low, largest):
    gain, own = 1.0, jax.random.fold_in(key, 6)
    for position, shards_of in split:
        steps = jnp.exp(jax.random.uniform(jax.random.fold_in(own, position), (shards_of,), jnp.float32, low / len(split), largest / len(split)))
        gain = gain * jnp.repeat(steps, shape[position] // shards_of).reshape([-1 if axis == position else 1 for axis in range(len(shape))])
    return gain


def bell_draw(stream_key, dims, width, limit, cuts=(), dtype=jnp.bfloat16):
    factor_of = block_scale(stream_key, dims, cuts, -0.22, 0.18) if cuts else 1.0
    entries = jax.random.normal(stream_key, dims, jnp.float32) * width * factor_of
    return jnp.minimum(jnp.maximum(entries, -limit), limit).astype(dtype)


def setup_inputs(seed: int = 0) -> dict:
    key_list = jax.random.split(jax.random.key(seed), 10)
    return {
        "inputs": bell_draw(key_list[0], (SEQS, LEN, D), 1.0, 6.0, ((1, 64), (2, 4))),
        "mix_first": bell_draw(key_list[1], (NA, BLK, BLK), BLK ** -0.5, 0.375, ((0, 64),)),
        "mix_second": bell_draw(key_list[2], (BLK, NA, NA), NA ** -0.5, 0.375, ((0, 64),)),
        "gate_scale": jnp.clip(jnp.exp(math.log(2.0) - 1.3862944 * jax.random.uniform(key_list[3], (D,), jnp.float32) ** block_scale(key_list[3], (D,), ((0, 4),), -0.2, 0.2)), 0.5, 2.0),
        "gate_bias": bell_draw(key_list[4], (D,), 1.0, 3.0, ((0, 4),), jnp.float32),
        "up_first": bell_draw(key_list[5], (NC, CB, CB), CB ** -0.5, 0.25, ((0, 4),)),
        "up_second": bell_draw(key_list[6], (NC, HB, CB), CB ** -0.5, 0.25, ((0, 4),)),
        "down_first": bell_draw(key_list[7], (NC, CB, HB), HB ** -0.5, 0.125, ((0, 4),)),
        "down_second": bell_draw(key_list[8], (NC, CB, CB), CB ** -0.5, 0.25, ((0, 4),)),
    }


def monarch(values, inner_weight, outer_weight):
    block_count = inner_weight.shape[0]
    inner_width = inner_weight.shape[1]
    in_width = inner_weight.shape[2]
    out_width = outer_weight.shape[1]
    leading = values.shape[:-1]
    blocked = values.reshape(leading + (block_count, in_width)).astype(jnp.float32)
    inner_rows = jnp.einsum('cqp,...cp->...cq', inner_weight.astype(jnp.float32), blocked).astype(jnp.bfloat16)
    permuted = jnp.swapaxes(inner_rows, -1, -2).reshape(leading + (block_count, inner_width)).astype(jnp.float32)
    projected = jnp.einsum('lor,...lr->...lo', outer_weight.astype(jnp.float32), permuted)
    return projected.reshape(leading + (block_count * out_width,))


def reference(inputs, mix_first, mix_second, gate_scale, gate_bias, up_first, up_second, down_first, down_second):
    def one_sequence(tokens):
        grouped = tokens.reshape(NA, BLK, D).astype(jnp.float32)
        first_pass = jnp.einsum('abq,aqd->abd', mix_first.astype(jnp.float32), grouped).astype(jnp.bfloat16)
        mixed_rows = jnp.einsum('bxy,ybd->xbd', mix_second.astype(jnp.float32), first_pass.astype(jnp.float32))
        mixed_rows = mixed_rows.astype(jnp.bfloat16).reshape(LEN, D).astype(jnp.float32)
        residual_in = tokens.astype(jnp.float32)
        hidden = (residual_in + mixed_rows * jax.nn.sigmoid(gate_scale * residual_in + gate_bias)).astype(jnp.bfloat16)
        expanded = monarch(hidden, up_first, up_second)
        activated = jax.nn.gelu(expanded, approximate=True).astype(jnp.bfloat16)
        contracted = monarch(activated, down_first, down_second)
        return (hidden.astype(jnp.float32) + contracted).astype(jnp.bfloat16)

    return lax.map(one_sequence, inputs)
```

```python
import functools

import jax
import jax.numpy as jnp
from jax import lax
from jax.experimental import pallas as pl
from jax.experimental.pallas import tpu as pltpu
from jax.sharding import PartitionSpec as P

BF16 = jnp.bfloat16
F32 = jnp.float32
BOTH = ("seq", "chan")
MIB = 1 << 20
VMEM = pl.BlockSpec(memory_space=pltpu.VMEM)
HBM = pl.BlockSpec(memory_space=pl.ANY)


def params(mib):
    return pltpu.CompilerParams(vmem_limit_bytes=mib * MIB)


def mm(a, b):
    return jnp.dot(a, b, preferred_element_type=F32)


def mm_nt(a, b):
    return lax.dot_general(a, b, (((1,), (1,)), ((), ())), preferred_element_type=F32)


def iota2(shape, axis):
    return lax.broadcasted_iota(jnp.int32, shape, axis)


def one_hot(shape, pick):
    return jnp.where(pick(iota2(shape, 0), iota2(shape, 1)), 1.0, 0.0).astype(BF16)


def first_kernel(x_ref, m_ref, o_ref, acc):
    for a in range(4):
        for s in range(2):
            acc[:, s * 4 + a, :] = mm(m_ref[a], x_ref[s, a])
    o_ref[...] = acc[...].reshape(64, 32, 512).astype(BF16)


def first_mix(x, m):
    return pl.pallas_call(
        first_kernel,
        out_shape=jax.ShapeDtypeStruct((64, 32, 512), BF16),
        in_specs=[VMEM, VMEM],
        out_specs=VMEM,
        scratch_shapes=[pltpu.VMEM((256, 8, 512), F32)],
        compiler_params=params(32),
        cost_estimate=pl.CostEstimate(flops=2**29, bytes_accessed=5 * MIB, transcendentals=0),
        name="first_mix",
    )(x, m)


def spread_kernel(m_ref, o_ref):
    rows = one_hot((256, 256), lambda r, x: x == (r % 64) * 4 + r // 64)
    for b in range(4):
        turned = mm(rows, m_ref[b]).astype(BF16)
        for s in range(2):
            slot = (b % 2) * 2 + s
            place = one_hot(
                (256, 1024),
                lambda y, k: k == (y // 4) * 16 + (b % 2) * 8 + s * 4 + y % 4,
            )
            o_ref[b // 2, slot * 256 : (slot + 1) * 256, :] = mm(turned, place).astype(BF16)


def spread(m):
    return pl.pallas_call(
        spread_kernel,
        out_shape=jax.ShapeDtypeStruct((2, 1024, 1024), BF16),
        in_specs=[VMEM],
        out_specs=VMEM,
        compiler_params=params(32),
        cost_estimate=pl.CostEstimate(flops=2**30, bytes_accessed=5 * MIB, transcendentals=0),
        name="spread",
    )(m)


def second_kernel(r_ref, m_ref, o_ref, acc):
    for p in range(2):
        part = r_ref[:, p * 16 : (p + 1) * 16, :].reshape(1024, 512)
        for slot in range(4):
            b, s = p * 2 + slot // 2, slot % 2
            acc[:, s * 4 + b, :] = mm(m_ref[p, slot * 256 : (slot + 1) * 256, :], part)
    o_ref[...] = acc[...].astype(BF16)


def second_mix(received, m):
    return pl.pallas_call(
        second_kernel,
        out_shape=jax.ShapeDtypeStruct((256, 8, 512), BF16),
        in_specs=[VMEM, VMEM],
        out_specs=VMEM,
        scratch_shapes=[pltpu.VMEM((256, 8, 512), F32)],
        compiler_params=params(32),
        cost_estimate=pl.CostEstimate(flops=2**31, bytes_accessed=8 * MIB, transcendentals=0),
        name="second_mix",
    )(received, m)


def pack_kernel(w1, w2, w3, w4, o_ref):
    same = one_hot((512, 512), lambda r, c: r == c)
    turn = one_hot((512, 512), lambda k, m: m == (k % 128) * 4 + k // 128)
    o_ref[0:512, :] = mm_nt(same, w1[0]).astype(BF16)
    for j in range(4):
        lo = 512 + j * 512
        o_ref[lo : lo + 512, :] = mm_nt(turn, w2[0, j * 512 : (j + 1) * 512, :]).astype(BF16)
        lo = 2560 + j * 512
        o_ref[lo : lo + 512, :] = mm_nt(same, w3[0, :, j * 512 : (j + 1) * 512]).astype(BF16)
    o_ref[4608:5120, :] = mm_nt(turn, w4[0]).astype(BF16)


def pack(w1, w2, w3, w4):
    return pl.pallas_call(
        pack_kernel,
        out_shape=jax.ShapeDtypeStruct((5120, 512), BF16),
        in_specs=[VMEM] * 4,
        out_specs=VMEM,
        compiler_params=params(32),
        cost_estimate=pl.CostEstimate(flops=2**31, bytes_accessed=10 * MIB, transcendentals=0),
        name="pack",
    )(w1, w2, w3, w4)


def mlp_kernel(
    meta, r_hbm, x0, x1, x2, x3, gs_ref, gb_ref, w_own, w_core,
    n0, n1, n2, n3, c0, c1, c2, c3, o_ref,
    rec, xin, wts, hid, mid, mid2, rec_sem, x_sem, w_sem,
):
    chan, y = meta[0], meta[1]
    copies = [pltpu.make_async_copy(r_hbm, rec, rec_sem)]
    for k, src in enumerate((x0, x1, x2, x3)):
        copies.append(pltpu.make_async_copy(src, xin.at[chan ^ k], x_sem.at[k]))
    weights = [
        pltpu.make_async_copy(w_own, wts.at[chan], w_sem.at[0]),
        pltpu.make_async_copy(w_core, wts.at[chan ^ 1], w_sem.at[1]),
    ]
    for flip, pieces in ((2, (n0, n1, n2, n3)), (3, (c0, c1, c2, c3))):
        for src, off in zip(pieces, (0, 3, 1, 2)):
            lo = pl.multiple_of(((y + off) % 4) * 1280, 1280)
            sem = w_sem.at[len(weights)]
            weights.append(
                pltpu.make_async_copy(src, wts.at[chan ^ flip, pl.ds(lo, 1280), :], sem)
            )
    for c in copies + weights:
        c.start()
    for c in copies:
        c.wait()
    order = one_hot(
        (512, 512),
        lambda r, k: k == ((r % 256) // 4) * 8 + (r // 256) * 4 + r % 4,
    )
    for c in range(4):
        lanes = slice(c * 512, (c + 1) * 512)
        mixed = mm(order, rec[c])
        res = xin[c].reshape(512, 512).astype(F32)
        z = gs_ref[0:1, lanes] * res + gb_ref[0:1, lanes]
        hid[:, lanes] = (res + mixed * (0.5 * jnp.tanh(0.5 * z) + 0.5)).astype(BF16)
    for c in weights:
        c.wait()
    for c in range(4):
        inner = mm(hid[:, c * 512 : (c + 1) * 512], wts[c, 0:512, :]).astype(BF16)
        for l in range(4):
            mid[l, :, c * 128 : (c + 1) * 128] = inner[:, l * 128 : (l + 1) * 128]
    for l in range(4):
        total = None
        for j in range(4):
            e = mm(mid[l], wts[l, 512 + j * 512 : 1024 + j * 512, :])
            u = e * (0.7978845608028654 + 0.035677408136300125 * (e * e))
            half = 0.5 * e
            act = (half + half * jnp.tanh(u)).astype(BF16)
            t = mm(act, wts[l, 2560 + j * 512 : 3072 + j * 512, :])
            total = t if total is None else total + t
        inner = total.astype(BF16)
        for k in range(4):
            mid2[k, :, l * 128 : (l + 1) * 128] = inner[:, k * 128 : (k + 1) * 128]
    for k in range(4):
        lanes = slice(k * 512, (k + 1) * 512)
        t = mm(mid2[k], wts[k, 4608:5120, :])
        o_ref[:, :, lanes] = (hid[:, lanes].astype(F32) + t).astype(BF16).reshape(2, 256, 512)


def mlp(meta, received, xs, gs, gb, w_own, w_core, near, cross):
    smem = pl.BlockSpec(memory_space=pltpu.SMEM)
    return pl.pallas_call(
        mlp_kernel,
        out_shape=jax.ShapeDtypeStruct((2, 256, 2048), BF16),
        in_specs=[smem] + [HBM] * 5 + [VMEM] * 2 + [HBM] * 10,
        out_specs=VMEM,
        scratch_shapes=[
            pltpu.VMEM((4, 512, 512), BF16),
            pltpu.VMEM((4, 2, 256, 512), BF16),
            pltpu.VMEM((4, 5120, 512), BF16),
            pltpu.VMEM((512, 2048), BF16),
            pltpu.VMEM((4, 512, 512), BF16),
            pltpu.VMEM((4, 512, 512), BF16),
            pltpu.SemaphoreType.DMA,
            pltpu.SemaphoreType.DMA((4,)),
            pltpu.SemaphoreType.DMA((10,)),
        ],
        compiler_params=params(52),
        cost_estimate=pl.CostEstimate(
            flops=11 * 2**30, bytes_accessed=26 * MIB, transcendentals=5 * MIB
        ),
        name="mlp",
    )(meta, received, *xs, gs, gb, w_own, w_core, *near, *cross)


def place(y, z, xl, h, c):
    return (((y % 4) * 8 + z) * 2 + xl) * 4 + h * 2 + c


def pairs(move):
    out = []
    for i in range(256):
        seq, chan = divmod(i, 4)
        y, rest = divmod(seq, 16)
        z, xl = divmod(rest, 2)
        out.append((i, place(*move(y, z, xl, chan // 2, chan % 2))))
    return out


def next_along_x(y, z, xl, h, c):
    return y, z, 1 - xl, 1 - h, c


TO_X = pairs(next_along_x)
TO_CORE = pairs(lambda y, z, xl, h, c: (y, z, xl, h, 1 - c))
TO_CHAN = [
    pairs(lambda y, z, xl, h, c, k=k: (y, z, xl, h ^ (k >> 1), c ^ (k & 1))) for k in range(4)
]


def along_y(step):
    return pairs(lambda y, z, xl, h, c: (y + step, z, xl, h, c))


def on_device(
    inputs, mix_first, mix_second, gate_scale, gate_bias, up_first, up_second, down_first, down_second
):
    chan = lax.axis_index("chan")
    y = lax.axis_index("seq") // 16
    meta = jnp.stack([chan, y]).astype(jnp.int32)
    grouped = inputs.reshape(2, 4, 256, 512)
    sent = first_mix(grouped, mix_first)
    received = lax.all_to_all(sent, "seq", split_axis=0, concat_axis=0, tiled=True)

    sent, up_first, mix_second = lax.optimization_barrier((sent, up_first, mix_second))
    spread_second = spread(mix_second)
    packed = pack(up_first, up_second, down_first, down_second)
    gates = lax.all_gather(jnp.stack([gate_scale, gate_bias]), "chan", axis=1, tiled=True)
    xs = []
    for k in range(4):
        part = lax.dynamic_index_in_dim(grouped, chan ^ k, 1, keepdims=False)
        xs.append(lax.ppermute(part, BOTH, TO_CHAN[k]) if k else part)
    quarter = lax.dynamic_slice_in_dim(packed, y * 1280, 1280, 0)
    near = [lax.ppermute(quarter, BOTH, TO_X)]
    near += [lax.ppermute(near[0], BOTH, along_y(step)) for step in (1, -1, 2)]
    w_core = lax.ppermute(packed, BOTH, TO_CORE)
    cross = [lax.ppermute(piece, BOTH, TO_CORE) for piece in near]

    sent2 = second_mix(received, spread_second)
    received2 = lax.all_to_all(sent2, ("chan", "seq"), split_axis=0, concat_axis=0, tiled=True)
    return mlp(
        meta, received2.reshape(4, 512, 512), xs, gates[0:1], gates[1:2], packed, w_core, near, cross
    )


def solution(mesh):
    return jax.shard_map(
        on_device,
        mesh=mesh,
        in_specs=(
            P(None, "seq", "chan"),
            P("seq", None, None),
            P("seq", None, None),
            P("chan"),
            P("chan"),
            P("chan", None, None),
            P("chan", None, None),
            P("chan", None, None),
            P("chan", None, None),
        ),
        out_specs=P(None, ("seq", "chan"), None),
        check_vma=False,
    )
```

```python
import functools

import jax
import jax.numpy as jnp
from jax import lax
from jax.experimental import pallas as pl
from jax.experimental.pallas import tpu as pltpu
from jax.sharding import PartitionSpec as P

BF16 = jnp.bfloat16
F32 = jnp.float32
BOTH = ("seq", "chan")
MIB = 1 << 20
FULL = 58
CUT = 256
VMEM = pl.BlockSpec(memory_space=pltpu.VMEM)
HBM = pl.BlockSpec(memory_space=pltpu.HBM)
SMEM = pl.BlockSpec(memory_space=pltpu.SMEM)


def params(mib):
    return pltpu.CompilerParams(vmem_limit_bytes=mib * MIB)


def mm(a, b):
    return jnp.dot(a, b, preferred_element_type=F32)


def mm_nt(a, b):
    return lax.dot_general(a, b, (((1,), (1,)), ((), ())), preferred_element_type=F32)


def iota2(shape, axis):
    return lax.broadcasted_iota(jnp.int32, shape, axis)


def one_hot(shape, pick):
    return jnp.where(pick(iota2(shape, 0), iota2(shape, 1)), 1.0, 0.0).astype(BF16)


def first_kernel(lo, hi, meta, x_hbm, m_hbm, o_ref, acc, x, m, sems):
    copies = []
    for a in range(4):
        copies.append(
            (
                pltpu.make_async_copy(m_hbm.at[a], m.at[a], sems.at[2 * a]),
                pltpu.make_async_copy(x_hbm.at[:, a, :, lo:hi], x.at[a], sems.at[2 * a + 1]),
            )
        )
    for pair in copies:
        for c in pair:
            c.start()
    for a in range(4):
        for c in copies[a]:
            c.wait()
        for s in range(2):
            acc[:, s * 4 + a, :] = mm(m[a], x[a, s])
    o_ref[...] = acc[...].reshape(64, 32, hi - lo).astype(BF16)


def first_mix(lo, hi, meta, x, m):
    lanes = hi - lo
    return pl.pallas_call(
        functools.partial(first_kernel, lo, hi),
        out_shape=jax.ShapeDtypeStruct((64, 32, lanes), BF16),
        in_specs=[SMEM, HBM, HBM],
        out_specs=VMEM,
        scratch_shapes=[
            pltpu.VMEM((256, 8, lanes), F32),
            pltpu.VMEM((4, 2, 256, lanes), BF16),
            pltpu.VMEM((4, 256, 256), BF16),
            pltpu.SemaphoreType.DMA((8,)),
        ],
        compiler_params=params(FULL),
        cost_estimate=pl.CostEstimate(flops=2**29, bytes_accessed=5 * MIB, transcendentals=0),
        name=f"first_mix_{lo}",
    )(meta, x, m)


def spread_kernel(meta, m_ref, o_ref):
    rows = one_hot((256, 256), lambda r, x: x == (r % 64) * 4 + r // 64)
    for b in range(4):
        turned = mm(rows, m_ref[b]).astype(BF16)
        for s in range(2):
            slot = (b % 2) * 2 + s
            place = one_hot(
                (256, 1024),
                lambda y, k: k == (y // 4) * 16 + (b % 2) * 8 + s * 4 + y % 4,
            )
            o_ref[b // 2, slot * 256 : (slot + 1) * 256, :] = mm(turned, place).astype(BF16)


def spread(meta, m):
    return pl.pallas_call(
        spread_kernel,
        out_shape=jax.ShapeDtypeStruct((2, 1024, 1024), BF16),
        in_specs=[SMEM, VMEM],
        out_specs=VMEM,
        compiler_params=params(FULL),
        cost_estimate=pl.CostEstimate(flops=2**30, bytes_accessed=5 * MIB, transcendentals=0),
        name="spread",
    )(meta, m)


def second_kernel(lo, hi, r_hbm, m_hbm, *refs):
    *before, o_ref, acc, r, m, sems = refs
    copies = []
    for p in range(2):
        rows = pl.ds(p * 16, 16)
        copies.append(pltpu.make_async_copy(r_hbm.at[:, rows, :], r.at[p], sems.at[2 * p]))
        copies.append(pltpu.make_async_copy(m_hbm.at[p], m.at[p], sems.at[2 * p + 1]))
    if before:
        copies.append(pltpu.make_async_copy(before[0], o_ref.at[:, :, 0:lo], sems.at[4]))
    for c in copies:
        c.start()
    for p in range(2):
        copies[2 * p].wait()
        copies[2 * p + 1].wait()
        part = r[p].reshape(1024, hi - lo)
        for slot in range(4):
            b, s = p * 2 + slot // 2, slot % 2
            acc[:, s * 4 + b, :] = mm(m[p, slot * 256 : (slot + 1) * 256, :], part)
    if before:
        copies[4].wait()
        o_ref[:, :, lo:hi] = acc[...].astype(BF16)
    else:
        o_ref[...] = acc[...].astype(BF16)


def second_mix(lo, hi, received, m, *before):
    lanes = hi - lo
    return pl.pallas_call(
        functools.partial(second_kernel, lo, hi),
        out_shape=jax.ShapeDtypeStruct((256, 8, hi if before else lanes), BF16),
        in_specs=[HBM] * (2 + len(before)),
        out_specs=VMEM,
        scratch_shapes=[
            pltpu.VMEM((256, 8, lanes), F32),
            pltpu.VMEM((2, 64, 16, lanes), BF16),
            pltpu.VMEM((2, 1024, 1024), BF16),
            pltpu.SemaphoreType.DMA((5,)),
        ],
        compiler_params=params(FULL),
        cost_estimate=pl.CostEstimate(flops=2**30, bytes_accessed=6 * MIB, transcendentals=0),
        name=f"second_mix_{lo}",
    )(received, m, *before)


A_ROWS, B_ROWS = 656, 640


def same_rows(n, first):
    return one_hot((n, 512), lambda r, c: c == r + first)


def turned_rows(n, first):
    return one_hot((n, 512), lambda r, m: m == ((r + first) % 128) * 4 + (r + first) // 128)


def gate_rows(g_ref):
    rows = []
    for v in range(2):
        rest = g_ref[v : v + 1, :]
        for _ in range(3):
            part = rest.astype(BF16).astype(F32)
            rows.append(part)
            rest = rest - part
    return jnp.concatenate(rows + [jnp.zeros((10, 512), F32)], axis=0).astype(BF16)


def quarter_kernel(meta, g_ref, w1, w2, w3, w4, a_ref, b_ref, v1, v2, v3, v4, sem):
    y = meta[1]
    lo = pl.multiple_of(y * 512, 512)
    copies = [
        pltpu.make_async_copy(w1.at[0], v1, sem.at[0]),
        pltpu.make_async_copy(w2.at[0, pl.ds(lo, 512), :], v2, sem.at[1]),
        pltpu.make_async_copy(w3.at[0, :, pl.ds(lo, 512)], v3, sem.at[2]),
        pltpu.make_async_copy(w4.at[0], v4, sem.at[3]),
    ]
    for c in copies:
        c.start()
    for c in copies:
        c.wait()
    a_ref[0:128, :] = mm_nt(same_rows(128, y * 128), v1[...]).astype(BF16)
    a_ref[128:640, :] = mm_nt(turned_rows(512, 0), v2[...]).astype(BF16)
    a_ref[640:656, :] = gate_rows(g_ref)
    b_ref[0:512, :] = mm_nt(same_rows(512, 0), v3[...]).astype(BF16)
    b_ref[512:640, :] = mm_nt(turned_rows(128, y * 128), v4[...]).astype(BF16)


def quarter(meta, gate, w1, w2, w3, w4):
    return pl.pallas_call(
        quarter_kernel,
        out_shape=(
            jax.ShapeDtypeStruct((A_ROWS, 512), BF16),
            jax.ShapeDtypeStruct((B_ROWS, 512), BF16),
        ),
        in_specs=[SMEM, VMEM] + [HBM] * 4,
        out_specs=(VMEM, VMEM),
        scratch_shapes=[pltpu.VMEM((512, 512), BF16)] * 4 + [pltpu.SemaphoreType.DMA((4,))],
        compiler_params=params(FULL),
        cost_estimate=pl.CostEstimate(flops=2**29, bytes_accessed=4 * MIB, transcendentals=0),
        name="quarter",
    )(meta, gate, w1, w2, w3, w4)


def pack_kernel(meta, g_ref, w1, w2, w3, w4, o_ref):
    same = same_rows(512, 0)
    turn = turned_rows(512, 0)
    first = mm_nt(same, w1[0]).astype(BF16)
    last = mm_nt(turn, w4[0]).astype(BF16)
    for j in range(4):
        wide = slice(j * 512, (j + 1) * 512)
        o_ref[j, 0:128, :] = first[j * 128 : (j + 1) * 128]
        o_ref[j, 128:640, :] = mm_nt(turn, w2[0, wide, :]).astype(BF16)
        o_ref[j, 640:656, :] = gate_rows(g_ref)
        o_ref[j, 656:1168, :] = mm_nt(same, w3[0, :, wide]).astype(BF16)
        o_ref[j, 1168:1296, :] = last[j * 128 : (j + 1) * 128]


def pack(meta, gate, w1, w2, w3, w4):
    return pl.pallas_call(
        pack_kernel,
        out_shape=jax.ShapeDtypeStruct((4, A_ROWS + B_ROWS, 512), BF16),
        in_specs=[SMEM] + [VMEM] * 5,
        out_specs=VMEM,
        compiler_params=params(FULL),
        cost_estimate=pl.CostEstimate(flops=2**31, bytes_accessed=10 * MIB, transcendentals=0),
        name="pack",
    )(meta, gate, w1, w2, w3, w4)


def mlp_kernel(
    meta, r_hbm, x0, x1, x2, x3, own, swapped, near_a, near_b, cross_a, cross_b,
    o_ref, rec, xin, gate, hid, mid, mid2, w1, w2, w3, w4, sems,
):
    chan = meta[0]
    waits = {}
    count = [0]

    def fetch(key, src, dst):
        copy = pltpu.make_async_copy(src, dst, sems.at[count[0]])
        count[0] += 1
        copy.start()
        waits.setdefault(key, []).append(copy)

    spans = ((0, 128), (128, 640), (640, 656), (656, 1168), (1168, 1296))

    def fetch_part(part, k):
        dst = (w1, w2, gate, w3, w4)[part]
        lo, hi = spans[part]
        block = chan ^ k
        if k < 2:
            src = (own, swapped)[k]
            if part == 2:
                fetch((part, k), src.at[0, lo:hi, :], dst.at[block])
            else:
                fetch((part, k), src.at[:, lo:hi, :], dst.at[block])
        else:
            first, last = (near_a, near_b) if k == 2 else (cross_a, cross_b)
            src, base = (first, 0) if part < 3 else (last, A_ROWS)
            if part == 2:
                fetch((part, k), src.at[0, lo - base : hi - base, :], dst.at[block])
            else:
                fetch((part, k), src.at[:, lo - base : hi - base, :], dst.at[block])

    def ready(part, k):
        for copy in waits[(part, k)]:
            copy.wait()

    for k, x_ref in enumerate((x0, x1, x2, x3)):
        fetch((5, k), r_hbm.at[chan ^ k], rec.at[k])
        fetch((5, k), x_ref, xin.at[k])
        fetch_part(2, k)
        fetch_part(0, k)
    for k in range(4):
        fetch_part(1, k)
        fetch_part(3, k)
    for k in range(4):
        fetch_part(4, k)

    order = one_hot(
        (512, 512),
        lambda r, k: k == ((r % 256) // 4) * 8 + (r // 256) * 4 + r % 4,
    )
    for k in range(4):
        c = chan ^ k
        ready(5, k)
        mixed = mm(order, rec[k])
        res = xin[k].reshape(512, 512).astype(F32)
        ready(2, k)
        g = gate[c].astype(F32)
        scale = (g[0:1] + g[1:2]) + g[2:3]
        bias = (g[3:4] + g[4:5]) + g[5:6]
        z = scale * res + bias
        hidden = (res + mixed * (0.5 * jnp.tanh(0.5 * z) + 0.5)).astype(BF16)
        hid[c] = hidden
        ready(0, k)
        inner = mm(hidden, w1[c].reshape(512, 512)).astype(BF16)
        for l in range(4):
            mid[l, c] = inner[:, l * 128 : (l + 1) * 128]
    for k in range(4):
        l = chan ^ k
        rows = jnp.concatenate([mid[l, c] for c in range(4)], axis=1)
        ready(1, k)
        ready(3, k)
        total = None
        for j in range(4):
            e = mm(rows, w2[l, j])
            u = e * (0.7978845608028654 + 0.035677408136300125 * (e * e))
            half = 0.5 * e
            act = (half + half * jnp.tanh(u)).astype(BF16)
            t = mm(act, w3[l, j])
            total = t if total is None else total + t
        inner = total.astype(BF16)
        for n in range(4):
            mid2[n, l] = inner[:, n * 128 : (n + 1) * 128]
    for k in range(4):
        n = chan ^ k
        rows = jnp.concatenate([mid2[n, l] for l in range(4)], axis=1)
        ready(4, k)
        t = mm(rows, w4[n].reshape(512, 512))
        out = (hid[n].astype(F32) + t).astype(BF16)
        o_ref[:, :, pl.ds(pl.multiple_of(n * 512, 512), 512)] = out.reshape(2, 256, 512)


def mlp(meta, received, xs, own, swapped, near, cross):
    wide = pltpu.VMEM((4, 4, 512, 512), BF16)
    narrow = pltpu.VMEM((4, 4, 128, 512), BF16)
    tall = pltpu.VMEM((4, 4, 512, 128), BF16)
    return pl.pallas_call(
        mlp_kernel,
        out_shape=jax.ShapeDtypeStruct((2, 256, 2048), BF16),
        in_specs=[SMEM] + [HBM] * 11,
        out_specs=VMEM,
        scratch_shapes=[
            pltpu.VMEM((4, 512, 512), BF16),
            pltpu.VMEM((4, 2, 256, 512), BF16),
            pltpu.VMEM((4, 16, 512), BF16),
            pltpu.VMEM((4, 512, 512), BF16),
            tall,
            tall,
            narrow,
            wide,
            wide,
            narrow,
            pltpu.SemaphoreType.DMA((28,)),
        ],
        compiler_params=params(FULL),
        cost_estimate=pl.CostEstimate(
            flops=11 * 2**30, bytes_accessed=26 * MIB, transcendentals=5 * MIB
        ),
        name="mlp",
    )(meta, received, *xs, own, swapped, *near, *cross)


def place(y, z, xl, h, c):
    return (((y % 4) * 8 + z) * 2 + xl) * 4 + h * 2 + c


def pairs(move):
    out = []
    for i in range(256):
        seq, chan = divmod(i, 4)
        y, rest = divmod(seq, 16)
        z, xl = divmod(rest, 2)
        out.append((i, place(*move(y, z, xl, chan // 2, chan % 2))))
    return out


def next_along_x(y, z, xl, h, c):
    return y, z, 1 - xl, 1 - h, c


TO_X = pairs(next_along_x)
TO_CORE = pairs(lambda y, z, xl, h, c: (y, z, xl, h, 1 - c))
TO_CHAN = [
    pairs(lambda y, z, xl, h, c, k=k: (y, z, xl, h ^ (k >> 1), c ^ (k & 1))) for k in range(4)
]


RINGS = [[y * 16 + rest for y in range(4)] for rest in range(16)]


def gather_ring(piece):
    out = lax.all_gather(piece, "seq", axis_index_groups=RINGS, axis=0, tiled=True)
    return out.reshape(4, *piece.shape)


def on_device(
    inputs, mix_first, mix_second, gate_scale, gate_bias, up_first, up_second, down_first, down_second
):
    bar = lax.optimization_barrier
    chan = lax.axis_index("chan")
    y = lax.axis_index("seq") // 16
    meta = jnp.stack([chan, y]).astype(jnp.int32)
    gate = jnp.stack([gate_scale, gate_bias])
    grouped = inputs.reshape(2, 4, 256, 512)
    to_b = lambda sent: lax.all_to_all(sent, "seq", split_axis=0, concat_axis=0, tiled=True)
    move = lambda piece, to: lax.ppermute(piece, BOTH, to)

    sent0 = first_mix(0, CUT, meta, grouped, mix_first)
    received0 = to_b(sent0)
    _, meta = bar((sent0, meta))
    mine_a, mine_b = quarter(meta, gate, up_first, up_second, down_first, down_second)
    near_a, near_b = move(mine_a, TO_X), move(mine_b, TO_X)
    _, meta = bar((mine_a, meta))
    sent1 = first_mix(CUT, 512, meta, grouped, mix_first)
    received0, near_a, sent1, meta = bar((received0, near_a, sent1, meta))
    received1 = to_b(sent1)
    near_a = gather_ring(near_a)
    spread_second = spread(meta, mix_second)
    own = pack(meta, gate, up_first, up_second, down_first, down_second)
    turned0 = second_mix(0, CUT, received0, spread_second)
    received1, spread_second, turned0, near_b, own, meta = bar(
        (received1, spread_second, turned0, near_b, own, meta)
    )
    near_b = gather_ring(near_b)
    turned = second_mix(CUT, 512, received1, spread_second, turned0)
    back = lax.all_to_all(turned, ("chan", "seq"), split_axis=0, concat_axis=0, tiled=True)
    _, own, meta = bar((turned, own, meta))
    xs = []
    for k in range(4):
        part = lax.dynamic_index_in_dim(grouped, meta[0] ^ k, 1, keepdims=False)
        xs.append(move(part, TO_CHAN[k]) if k else part)
    swapped, cross_a = move(own, TO_CORE), move(near_a, TO_CORE)
    near_b, xs, swapped, cross_a = bar((near_b, xs, swapped, cross_a))
    near, cross = [near_a, near_b], [cross_a, move(near_b, TO_CORE)]
    return mlp(meta, back.reshape(4, 512, 512), xs, own, swapped, near, cross)


def solution(mesh):
    return jax.shard_map(
        on_device,
        mesh=mesh,
        in_specs=(
            P(None, "seq", "chan"),
            P("seq", None, None),
            P("seq", None, None),
            P("chan"),
            P("chan"),
            P("chan", None, None),
            P("chan", None, None),
            P("chan", None, None),
            P("chan", None, None),
        ),
        out_specs=P(None, ("seq", "chan"), None),
        check_vma=False,
    )
```

```python
import functools

import jax
import jax.numpy as jnp
from jax import lax
from jax.experimental import pallas as pl
from jax.experimental.pallas import tpu as pltpu
from jax.sharding import PartitionSpec as P

BF16 = jnp.bfloat16
F32 = jnp.float32
BOTH = ("seq", "chan")
MIB = 1 << 20
FULL = 58
VMEM = pl.BlockSpec(memory_space=pltpu.VMEM)
HBM = pl.BlockSpec(memory_space=pltpu.HBM)
SMEM = pl.BlockSpec(memory_space=pltpu.SMEM)


def params(mib):
    return pltpu.CompilerParams(vmem_limit_bytes=mib * MIB)


def mm(a, b):
    return jnp.dot(a, b, preferred_element_type=F32)


def mm_nt(a, b):
    return lax.dot_general(a, b, (((1,), (1,)), ((), ())), preferred_element_type=F32)


def iota2(shape, axis):
    return lax.broadcasted_iota(jnp.int32, shape, axis)


def one_hot(shape, pick):
    return jnp.where(pick(iota2(shape, 0), iota2(shape, 1)), 1.0, 0.0).astype(BF16)


def first_kernel(x_hbm, m_hbm, o_ref, acc, x, m, sems):
    copies = []
    for a in range(4):
        copies.append(
            (
                pltpu.make_async_copy(m_hbm.at[a], m.at[a], sems.at[2 * a]),
                pltpu.make_async_copy(x_hbm.at[:, a], x.at[a], sems.at[2 * a + 1]),
            )
        )
    for pair in copies:
        for c in pair:
            c.start()
    for a in range(4):
        for c in copies[a]:
            c.wait()
        for s in range(2):
            acc[:, s * 4 + a, :] = mm(m[a], x[a, s])
    o_ref[...] = acc[...].reshape(64, 32, 512).astype(BF16)


def first_mix(x, m):
    return pl.pallas_call(
        first_kernel,
        out_shape=jax.ShapeDtypeStruct((64, 32, 512), BF16),
        in_specs=[HBM, HBM],
        out_specs=VMEM,
        scratch_shapes=[
            pltpu.VMEM((256, 8, 512), F32),
            pltpu.VMEM((4, 2, 256, 512), BF16),
            pltpu.VMEM((4, 256, 256), BF16),
            pltpu.SemaphoreType.DMA((8,)),
        ],
        compiler_params=params(FULL),
        cost_estimate=pl.CostEstimate(flops=2**29, bytes_accessed=5 * MIB, transcendentals=0),
        name="first_mix",
    )(x, m)


def spread_kernel(meta, m_ref, o_ref):
    rows = one_hot((256, 256), lambda r, x: x == (r % 64) * 4 + r // 64)
    for b in range(4):
        turned = mm(rows, m_ref[b]).astype(BF16)
        for s in range(2):
            slot = (b % 2) * 2 + s
            place = one_hot(
                (256, 1024),
                lambda y, k: k == (y // 4) * 16 + (b % 2) * 8 + s * 4 + y % 4,
            )
            o_ref[b // 2, slot * 256 : (slot + 1) * 256, :] = mm(turned, place).astype(BF16)


def spread(meta, m):
    return pl.pallas_call(
        spread_kernel,
        out_shape=jax.ShapeDtypeStruct((2, 1024, 1024), BF16),
        in_specs=[SMEM, VMEM],
        out_specs=VMEM,
        compiler_params=params(FULL),
        cost_estimate=pl.CostEstimate(flops=2**30, bytes_accessed=5 * MIB, transcendentals=0),
        name="spread",
    )(meta, m)


def second_kernel(r_hbm, m_hbm, o_ref, acc, r, m, sems):
    copies = []
    for p in range(2):
        rows = pl.ds(p * 16, 16)
        copies.append(pltpu.make_async_copy(r_hbm.at[:, rows, :], r.at[p], sems.at[2 * p]))
        copies.append(pltpu.make_async_copy(m_hbm.at[p], m.at[p], sems.at[2 * p + 1]))
    for c in copies:
        c.start()
    for p in range(2):
        copies[2 * p].wait()
        copies[2 * p + 1].wait()
        part = r[p].reshape(1024, 512)
        for slot in range(4):
            b, s = p * 2 + slot // 2, slot % 2
            acc[:, s * 4 + b, :] = mm(m[p, slot * 256 : (slot + 1) * 256, :], part)
    o_ref[...] = acc[...].astype(BF16)


def second_mix(received, m):
    return pl.pallas_call(
        second_kernel,
        out_shape=jax.ShapeDtypeStruct((256, 8, 512), BF16),
        in_specs=[HBM, HBM],
        out_specs=VMEM,
        scratch_shapes=[
            pltpu.VMEM((256, 8, 512), F32),
            pltpu.VMEM((2, 64, 16, 512), BF16),
            pltpu.VMEM((2, 1024, 1024), BF16),
            pltpu.SemaphoreType.DMA((4,)),
        ],
        compiler_params=params(FULL),
        cost_estimate=pl.CostEstimate(flops=2**31, bytes_accessed=8 * MIB, transcendentals=0),
        name="second_mix",
    )(received, m)


A_ROWS, B_ROWS = 656, 640


def same_rows(n, first):
    return one_hot((n, 512), lambda r, c: c == r + first)


def turned_rows(n, first):
    return one_hot((n, 512), lambda r, m: m == ((r + first) % 128) * 4 + (r + first) // 128)


def gate_rows(g_ref):
    rows = []
    for v in range(2):
        rest = g_ref[v : v + 1, :]
        for _ in range(3):
            part = rest.astype(BF16).astype(F32)
            rows.append(part)
            rest = rest - part
    return jnp.concatenate(rows + [jnp.zeros((10, 512), F32)], axis=0).astype(BF16)


def quarter_kernel(meta, g_ref, w1, w2, w3, w4, a_ref, b_ref, f_ref, v1, v2, v3, v5, v4, sem):
    y = meta[1]
    far = (y + 2) % 4
    near_at, far_at = pl.multiple_of(y * 512, 512), pl.multiple_of(far * 512, 512)
    copies = [
        pltpu.make_async_copy(w1.at[0], v1, sem.at[0]),
        pltpu.make_async_copy(w2.at[0, pl.ds(near_at, 512), :], v2, sem.at[1]),
        pltpu.make_async_copy(w3.at[0, :, pl.ds(near_at, 512)], v3, sem.at[2]),
        pltpu.make_async_copy(w3.at[0, :, pl.ds(far_at, 512)], v5, sem.at[3]),
        pltpu.make_async_copy(w4.at[0], v4, sem.at[4]),
    ]
    for c in copies:
        c.start()
    for c in copies:
        c.wait()
    a_ref[0:128, :] = mm_nt(same_rows(128, y * 128), v1[...]).astype(BF16)
    a_ref[128:640, :] = mm_nt(turned_rows(512, 0), v2[...]).astype(BF16)
    a_ref[640:656, :] = gate_rows(g_ref)
    for at, v, out in ((y, v3, b_ref), (far, v5, f_ref)):
        out[0:512, :] = mm_nt(same_rows(512, 0), v[...]).astype(BF16)
        out[512:640, :] = mm_nt(turned_rows(128, at * 128), v4[...]).astype(BF16)


def quarter(meta, gate, w1, w2, w3, w4):
    b_piece = jax.ShapeDtypeStruct((B_ROWS, 512), BF16)
    return pl.pallas_call(
        quarter_kernel,
        out_shape=(jax.ShapeDtypeStruct((A_ROWS, 512), BF16), b_piece, b_piece),
        in_specs=[SMEM, VMEM] + [HBM] * 4,
        out_specs=(VMEM, VMEM, VMEM),
        scratch_shapes=[pltpu.VMEM((512, 512), BF16)] * 5 + [pltpu.SemaphoreType.DMA((5,))],
        compiler_params=params(FULL),
        cost_estimate=pl.CostEstimate(flops=2**29, bytes_accessed=4 * MIB, transcendentals=0),
        name="quarter",
    )(meta, gate, w1, w2, w3, w4)


def pack_kernel(meta, g_ref, w1, w2, w3, w4, *o_refs):
    same = same_rows(512, 0)
    turn = turned_rows(512, 0)
    first = mm_nt(same, w1[0]).astype(BF16)
    last = mm_nt(turn, w4[0]).astype(BF16)
    for j in range(4):
        wide = slice(j * 512, (j + 1) * 512)
        o_refs[j][0:128, :] = first[j * 128 : (j + 1) * 128]
        o_refs[j][128:640, :] = mm_nt(turn, w2[0, wide, :]).astype(BF16)
        o_refs[j][640:656, :] = gate_rows(g_ref)
        o_refs[j][656:1168, :] = mm_nt(same, w3[0, :, wide]).astype(BF16)
        o_refs[j][1168:1296, :] = last[j * 128 : (j + 1) * 128]


def pack(meta, gate, w1, w2, w3, w4):
    return pl.pallas_call(
        pack_kernel,
        out_shape=(jax.ShapeDtypeStruct((A_ROWS + B_ROWS, 512), BF16),) * 4,
        in_specs=[SMEM] + [VMEM] * 5,
        out_specs=(VMEM,) * 4,
        compiler_params=params(FULL),
        cost_estimate=pl.CostEstimate(flops=2**31, bytes_accessed=10 * MIB, transcendentals=0),
        name="pack",
    )(meta, gate, w1, w2, w3, w4)


LOW = 320
PIECES = (
    (0, 656, 0),
    (0, 656, 3),
    (0, 656, 1),
    (0, LOW, 2),
    (LOW, 656, 2),
    (656, 1296, 0),
    (656, 1296, 3),
    (656, 1296, 1),
    (656, 1296, 2),
)
SPANS = ((0, 128), (128, 640), (640, 656), (656, 1168), (1168, 1296))


def mlp_kernel(
    meta, r_hbm, x0, x1, x2, x3, *refs
):
    own, swapped, refs = refs[:4], refs[4:8], refs[8:]
    pieces, refs = (refs[:9], refs[9:18]), refs[18:]
    o_hbm, act, out, rec, xin, gate, hid, mid, mid2, w1, w2, w3, w4, sems, o_sems = refs
    chan, y = meta[0], meta[1]
    waits = {}
    count = [0]

    def fetch(key, src, dst):
        copy = pltpu.make_async_copy(src, dst, sems.at[count[0]])
        count[0] += 1
        copy.start()
        waits.setdefault(key, []).append(copy)

    def fetch_part(part, k):
        dst = (w1, w2, gate, w3, w4)[part]
        lo, hi = SPANS[part]
        block = chan ^ k
        if k < 2:
            for j in range(1 if part == 2 else 4):
                to = dst.at[block] if part == 2 else dst.at[block, j]
                fetch((part, k), (own, swapped)[k][j].at[lo:hi, :], to)
        else:
            for src, (first, end, offset) in zip(pieces[k - 2], PIECES):
                a, b = max(lo, first), min(hi, end)
                if a >= b or (part == 2 and offset):
                    continue
                to = dst.at[block]
                if part != 2:
                    to = dst.at[block, (y + offset) % 4, a - lo : b - lo, :]
                fetch((part, k), src.at[a - first : b - first, :], to)

    def ready(part, k):
        for copy in waits[(part, k)]:
            copy.wait()

    def fetch_rows(k):
        fetch((5, k), r_hbm.at[chan ^ k], rec.at[k])
        fetch((5, k), (x0, x1, x2, x3)[k], xin.at[k])
        fetch_part(2, k)
        fetch_part(0, k)

    fetch_rows(0)
    fetch_rows(1)
    order = one_hot(
        (512, 512),
        lambda r, k: k == ((r % 256) // 4) * 8 + (r // 256) * 4 + r % 4,
    )
    for k in range(4):
        if k < 2:
            fetch_rows(k + 2)
        else:
            fetch_part(1, k - 2)
            fetch_part(3, k - 2)
        c = chan ^ k
        ready(5, k)
        mixed = mm(order, rec[k])
        res = xin[k].reshape(512, 512).astype(F32)
        ready(2, k)
        g = gate[c].astype(F32)
        scale = (g[0:1] + g[1:2]) + g[2:3]
        bias = (g[3:4] + g[4:5]) + g[5:6]
        z = scale * res + bias
        hidden = (res + mixed * (0.5 * jnp.tanh(0.5 * z) + 0.5)).astype(BF16)
        hid[c] = hidden
        ready(0, k)
        inner = mm(hidden, w1[c].reshape(512, 512)).astype(BF16)
        for l in range(4):
            mid[l, c] = inner[:, l * 128 : (l + 1) * 128]
    for k in range(4):
        if k < 2:
            fetch_part(1, k + 2)
            fetch_part(3, k + 2)
        else:
            fetch_part(4, 2 * k - 4)
            fetch_part(4, 2 * k - 3)
        l = chan ^ k
        rows = jnp.concatenate([mid[l, c] for c in range(4)], axis=1)
        ready(1, k)
        for j in range(4):
            e = mm(rows, w2[l, j])
            u = e * (0.7978845608028654 + 0.035677408136300125 * (e * e))
            half = 0.5 * e
            act[:, j * 512 : (j + 1) * 512] = (half + half * jnp.tanh(u)).astype(BF16)
        ready(3, k)
        inner = mm(act[...], w3[l].reshape(2048, 512)).astype(BF16)
        for n in range(4):
            mid2[n, l] = inner[:, n * 128 : (n + 1) * 128]
    stores = []
    for k in range(4):
        n = chan ^ k
        rows = jnp.concatenate([mid2[n, l] for l in range(4)], axis=1)
        ready(4, k)
        t = mm(rows, w4[n].reshape(512, 512))
        out[k] = (hid[n].astype(F32) + t).astype(BF16).reshape(2, 256, 512)
        lanes = pl.ds(pl.multiple_of(n * 512, 512), 512)
        stores.append(pltpu.make_async_copy(out.at[k], o_hbm.at[:, :, lanes], o_sems.at[k]))
        stores[k].start()
    for copy in stores:
        copy.wait()


def mlp(meta, received, xs, own, swapped, near, cross):
    wide = pltpu.VMEM((4, 4, 512, 512), BF16)
    narrow = pltpu.VMEM((4, 4, 128, 512), BF16)
    tall = pltpu.VMEM((4, 4, 512, 128), BF16)
    square = pltpu.VMEM((4, 512, 512), BF16)
    halves = pltpu.VMEM((4, 2, 256, 512), BF16)
    return pl.pallas_call(
        mlp_kernel,
        out_shape=jax.ShapeDtypeStruct((2, 256, 2048), BF16),
        in_specs=[SMEM] + [HBM] * 31,
        out_specs=HBM,
        scratch_shapes=[
            pltpu.VMEM((512, 2048), BF16),
            halves,
            square,
            halves,
            pltpu.VMEM((4, 16, 512), BF16),
            square,
            tall,
            tall,
            narrow,
            wide,
            wide,
            narrow,
            pltpu.SemaphoreType.DMA((80,)),
            pltpu.SemaphoreType.DMA((4,)),
        ],
        compiler_params=params(FULL),
        cost_estimate=pl.CostEstimate(
            flops=11 * 2**30, bytes_accessed=26 * MIB, transcendentals=5 * MIB
        ),
        name="mlp",
    )(meta, received, *xs, *own, *swapped, *near, *cross)


def place(y, z, xl, h, c):
    return (((y % 4) * 8 + z) * 2 + xl) * 4 + h * 2 + c


def pairs(move):
    out = []
    for i in range(256):
        seq, chan = divmod(i, 4)
        y, rest = divmod(seq, 16)
        z, xl = divmod(rest, 2)
        out.append((i, place(*move(y, z, xl, chan // 2, chan % 2))))
    return out


def next_along_x(y, z, xl, h, c):
    return y, z, 1 - xl, 1 - h, c


TO_X = pairs(next_along_x)
TO_CORE = pairs(lambda y, z, xl, h, c: (y, z, xl, h, 1 - c))
TO_CHAN = [
    pairs(lambda y, z, xl, h, c, k=k: (y, z, xl, h ^ (k >> 1), c ^ (k & 1))) for k in range(4)
]


def along_y(step):
    return pairs(lambda y, z, xl, h, c: (y + step, z, xl, h, c))


def on_device(
    inputs, mix_first, mix_second, gate_scale, gate_bias, up_first, up_second, down_first, down_second
):
    bar = lax.optimization_barrier
    chan = lax.axis_index("chan")
    y = lax.axis_index("seq") // 16
    meta = jnp.stack([chan, y]).astype(jnp.int32)
    gate = jnp.stack([gate_scale, gate_bias])
    grouped = inputs.reshape(2, 4, 256, 512)
    move = lambda piece, to: lax.ppermute(piece, BOTH, to)
    swap = lambda piece: lax.ppermute(piece, BOTH, TO_CORE)

    sent = first_mix(grouped, mix_first)
    received = lax.all_to_all(sent, "seq", split_axis=0, concat_axis=0, tiled=True)
    _, meta = bar((sent, meta))
    mine_a, mine_b, mine_far = quarter(meta, gate, up_first, up_second, down_first, down_second)
    _, meta = bar((mine_a, meta))
    near_a, near_b = move(mine_a, TO_X), move(mine_b, TO_X)
    _, mine_far = bar((near_b, mine_far))
    far_b = move(mine_far, TO_X)
    up_a, down_a = move(near_a, along_y(1)), move(near_a, along_y(-1))
    own = pack(meta, gate, up_first, up_second, down_first, down_second)
    swapped = [swap(piece) for piece in own]
    cross_near = [swap(near_a), swap(near_b)]
    spread_second = spread(meta, mix_second)
    received, spread_second, near_a, near_b, far_b, up_a, down_a, own, meta = bar(
        (received, spread_second, near_a, near_b, far_b, up_a, down_a, own, meta)
    )
    turned = second_mix(received, spread_second)
    back = lax.all_to_all(turned, ("chan", "seq"), split_axis=0, concat_axis=0, tiled=True)
    _, near_b, up_a, down_a, far_b, meta, swapped, cross_near = bar(
        (turned, near_b, up_a, down_a, far_b, meta, swapped, cross_near)
    )
    xs = []
    for k in range(4):
        part = lax.dynamic_index_in_dim(grouped, meta[0] ^ k, 1, keepdims=False)
        xs.append(move(part, TO_CHAN[k]) if k else part)
    up_b, down_b = move(near_b, along_y(1)), move(near_b, along_y(-1))
    low, high = move(up_a[:LOW], along_y(1)), move(down_a[LOW:], along_y(-1))
    xs, up_b, down_b, low, high, up_a, down_a, far_b = bar(
        (xs, up_b, down_b, low, high, up_a, down_a, far_b)
    )
    near = [near_a, up_a, down_a, low, high, near_b, up_b, down_b, far_b]
    cross = [cross_near[0]] + [swap(p) for p in near[1:5]]
    cross += [cross_near[1]] + [swap(p) for p in near[6:]]
    return mlp(meta, back.reshape(4, 512, 512), xs, own, swapped, near, cross)


def solution(mesh):
    return jax.shard_map(
        on_device,
        mesh=mesh,
        in_specs=(
            P(None, "seq", "chan"),
            P("seq", None, None),
            P("seq", None, None),
            P("chan"),
            P("chan"),
            P("chan", None, None),
            P("chan", None, None),
            P("chan", None, None),
            P("chan", None, None),
        ),
        out_specs=P(None, ("seq", "chan"), None),
        check_vma=False,
    )
```

```python
import functools

import jax
import jax.numpy as jnp
from jax import lax
from jax.experimental import pallas as pl
from jax.experimental.pallas import tpu as pltpu
from jax.sharding import PartitionSpec as P

BF16 = jnp.bfloat16
F32 = jnp.float32
BOTH = ("seq", "chan")
MIB = 1 << 20
FULL = 58
VMEM = pl.BlockSpec(memory_space=pltpu.VMEM)
HBM = pl.BlockSpec(memory_space=pltpu.HBM)
SMEM = pl.BlockSpec(memory_space=pltpu.SMEM)


def params(mib):
    return pltpu.CompilerParams(vmem_limit_bytes=mib * MIB)


def mm(a, b):
    return jnp.dot(a, b, preferred_element_type=F32)


def mm_nt(a, b):
    return lax.dot_general(a, b, (((1,), (1,)), ((), ())), preferred_element_type=F32)


def iota2(shape, axis):
    return lax.broadcasted_iota(jnp.int32, shape, axis)


def one_hot(shape, pick):
    return jnp.where(pick(iota2(shape, 0), iota2(shape, 1)), 1.0, 0.0).astype(BF16)


def first_kernel(x_hbm, m_hbm, o_ref, acc, x, m, sems):
    copies = []
    for a in range(4):
        copies.append(
            (
                pltpu.make_async_copy(m_hbm.at[a], m.at[a], sems.at[2 * a]),
                pltpu.make_async_copy(x_hbm.at[:, a], x.at[a], sems.at[2 * a + 1]),
            )
        )
    for pair in copies:
        for c in pair:
            c.start()
    for a in range(4):
        for c in copies[a]:
            c.wait()
        for s in range(2):
            acc[:, s * 4 + a, :] = mm(m[a], x[a, s])
    o_ref[...] = acc[...].reshape(64, 32, 512).astype(BF16)


def first_mix(x, m):
    return pl.pallas_call(
        first_kernel,
        out_shape=jax.ShapeDtypeStruct((64, 32, 512), BF16),
        in_specs=[HBM, HBM],
        out_specs=VMEM,
        scratch_shapes=[
            pltpu.VMEM((256, 8, 512), F32),
            pltpu.VMEM((4, 2, 256, 512), BF16),
            pltpu.VMEM((4, 256, 256), BF16),
            pltpu.SemaphoreType.DMA((8,)),
        ],
        compiler_params=params(FULL),
        cost_estimate=pl.CostEstimate(flops=2**29, bytes_accessed=5 * MIB, transcendentals=0),
        name="first_mix",
    )(x, m)


def spread_kernel(meta, m_ref, o_ref):
    rows = one_hot((256, 256), lambda r, x: x == (r % 64) * 4 + r // 64)
    for b in range(4):
        turned = mm(rows, m_ref[b]).astype(BF16)
        for s in range(2):
            slot = (b % 2) * 2 + s
            place = one_hot(
                (256, 1024),
                lambda y, k: k == (y // 4) * 16 + (b % 2) * 8 + s * 4 + y % 4,
            )
            o_ref[b // 2, slot * 256 : (slot + 1) * 256, :] = mm(turned, place).astype(BF16)


def spread(meta, m):
    return pl.pallas_call(
        spread_kernel,
        out_shape=jax.ShapeDtypeStruct((2, 1024, 1024), BF16),
        in_specs=[SMEM, VMEM],
        out_specs=VMEM,
        compiler_params=params(FULL),
        cost_estimate=pl.CostEstimate(flops=2**30, bytes_accessed=5 * MIB, transcendentals=0),
        name="spread",
    )(meta, m)


def second_kernel(r_hbm, m_hbm, o_ref, acc, r, m, sems):
    copies = []
    for p in range(2):
        rows = pl.ds(p * 16, 16)
        copies.append(pltpu.make_async_copy(r_hbm.at[:, rows, :], r.at[p], sems.at[2 * p]))
        copies.append(pltpu.make_async_copy(m_hbm.at[p], m.at[p], sems.at[2 * p + 1]))
    for c in copies:
        c.start()
    for p in range(2):
        copies[2 * p].wait()
        copies[2 * p + 1].wait()
        part = r[p].reshape(1024, 512)
        for slot in range(4):
            b, s = p * 2 + slot // 2, slot % 2
            acc[:, s * 4 + b, :] = mm(m[p, slot * 256 : (slot + 1) * 256, :], part)
    o_ref[...] = acc[...].astype(BF16)


def second_mix(received, m):
    return pl.pallas_call(
        second_kernel,
        out_shape=jax.ShapeDtypeStruct((256, 8, 512), BF16),
        in_specs=[HBM, HBM],
        out_specs=VMEM,
        scratch_shapes=[
            pltpu.VMEM((256, 8, 512), F32),
            pltpu.VMEM((2, 64, 16, 512), BF16),
            pltpu.VMEM((2, 1024, 1024), BF16),
            pltpu.SemaphoreType.DMA((4,)),
        ],
        compiler_params=params(34),
        cost_estimate=pl.CostEstimate(flops=2**31, bytes_accessed=8 * MIB, transcendentals=0),
        name="second_mix",
    )(received, m)


A_ROWS, B_ROWS = 656, 640


def same_rows(n, first):
    return one_hot((n, 512), lambda r, c: c == r + first)


def turned_rows(n, first):
    return one_hot((n, 512), lambda r, m: m == ((r + first) % 128) * 4 + (r + first) // 128)


def gate_rows(g_ref):
    rows = []
    for v in range(2):
        rest = g_ref[v : v + 1, :]
        for _ in range(3):
            part = rest.astype(BF16).astype(F32)
            rows.append(part)
            rest = rest - part
    return jnp.concatenate(rows + [jnp.zeros((10, 512), F32)], axis=0).astype(BF16)


def quarter_kernel(meta, g_ref, w1, w2, w3, w4, a_ref, b_ref, f_ref, v1, v2, v3, v5, v4, sem):
    y = meta[1]
    far = (y + 2) % 4
    near_at, far_at = pl.multiple_of(y * 512, 512), pl.multiple_of(far * 512, 512)
    copies = [
        pltpu.make_async_copy(w1.at[0], v1, sem.at[0]),
        pltpu.make_async_copy(w2.at[0, pl.ds(near_at, 512), :], v2, sem.at[1]),
        pltpu.make_async_copy(w3.at[0, :, pl.ds(near_at, 512)], v3, sem.at[2]),
        pltpu.make_async_copy(w3.at[0, :, pl.ds(far_at, 512)], v5, sem.at[3]),
        pltpu.make_async_copy(w4.at[0], v4, sem.at[4]),
    ]
    for c in copies:
        c.start()
    for c in copies:
        c.wait()
    a_ref[0:128, :] = mm_nt(same_rows(128, y * 128), v1[...]).astype(BF16)
    a_ref[128:640, :] = mm_nt(turned_rows(512, 0), v2[...]).astype(BF16)
    a_ref[640:656, :] = gate_rows(g_ref)
    for at, v, out in ((y, v3, b_ref), (far, v5, f_ref)):
        out[0:512, :] = mm_nt(same_rows(512, 0), v[...]).astype(BF16)
        out[512:640, :] = mm_nt(turned_rows(128, at * 128), v4[...]).astype(BF16)


def quarter(meta, gate, w1, w2, w3, w4):
    b_piece = jax.ShapeDtypeStruct((B_ROWS, 512), BF16)
    return pl.pallas_call(
        quarter_kernel,
        out_shape=(jax.ShapeDtypeStruct((A_ROWS, 512), BF16), b_piece, b_piece),
        in_specs=[SMEM, VMEM] + [HBM] * 4,
        out_specs=(VMEM, VMEM, VMEM),
        scratch_shapes=[pltpu.VMEM((512, 512), BF16)] * 5 + [pltpu.SemaphoreType.DMA((5,))],
        compiler_params=params(FULL),
        cost_estimate=pl.CostEstimate(flops=2**29, bytes_accessed=4 * MIB, transcendentals=0),
        name="quarter",
    )(meta, gate, w1, w2, w3, w4)


def pack_kernel(meta, g_ref, w1, w2, w3, w4, *o_refs):
    same = same_rows(512, 0)
    turn = turned_rows(512, 0)
    first = mm_nt(same, w1[0]).astype(BF16)
    last = mm_nt(turn, w4[0]).astype(BF16)
    for j in range(4):
        wide = slice(j * 512, (j + 1) * 512)
        o_refs[j][0:128, :] = first[j * 128 : (j + 1) * 128]
        o_refs[j][128:640, :] = mm_nt(turn, w2[0, wide, :]).astype(BF16)
        o_refs[j][640:656, :] = gate_rows(g_ref)
        o_refs[j][656:1168, :] = mm_nt(same, w3[0, :, wide]).astype(BF16)
        o_refs[j][1168:1296, :] = last[j * 128 : (j + 1) * 128]


def pack(meta, gate, w1, w2, w3, w4):
    return pl.pallas_call(
        pack_kernel,
        out_shape=(jax.ShapeDtypeStruct((A_ROWS + B_ROWS, 512), BF16),) * 4,
        in_specs=[SMEM] + [VMEM] * 5,
        out_specs=(VMEM,) * 4,
        compiler_params=params(FULL),
        cost_estimate=pl.CostEstimate(flops=2**31, bytes_accessed=10 * MIB, transcendentals=0),
        name="pack",
    )(meta, gate, w1, w2, w3, w4)


LOW = 320
PIECES = (
    (0, 656, 0),
    (0, 656, 3),
    (0, 656, 1),
    (0, LOW, 2),
    (LOW, 656, 2),
    (656, 1296, 0),
    (656, 1296, 3),
    (656, 1296, 1),
    (656, 1296, 2),
)
SPANS = ((0, 128), (128, 640), (640, 656), (656, 1168), (1168, 1296))


def mlp_kernel(
    meta, r_hbm, x0, x1, x2, x3, *refs
):
    own, swapped, refs = refs[:4], refs[4:8], refs[8:]
    pieces, refs = (refs[:9], refs[9:18]), refs[18:]
    o_hbm, act, out, rec, xin, gate, hid, mid, mid2, w1, w2, w3, w4, sems, o_sems = refs
    chan, y = meta[0], meta[1]
    waits = {}
    count = [0]

    def fetch(key, src, dst):
        copy = pltpu.make_async_copy(src, dst, sems.at[count[0]])
        count[0] += 1
        copy.start()
        waits.setdefault(key, []).append(copy)

    def fetch_part(part, k):
        dst = (w1, w2, gate, w3, w4)[part]
        lo, hi = SPANS[part]
        block = chan ^ k
        if k < 2:
            for j in range(1 if part == 2 else 4):
                to = dst.at[block] if part == 2 else dst.at[block, j]
                fetch((part, k), (own, swapped)[k][j].at[lo:hi, :], to)
        else:
            for src, (first, end, offset) in zip(pieces[k - 2], PIECES):
                a, b = max(lo, first), min(hi, end)
                if a >= b or (part == 2 and offset):
                    continue
                to = dst.at[block]
                if part != 2:
                    to = dst.at[block, (y + offset) % 4, a - lo : b - lo, :]
                fetch((part, k), src.at[a - first : b - first, :], to)

    def ready(part, k):
        for copy in waits[(part, k)]:
            copy.wait()

    def fetch_rows(k):
        fetch((5, k), r_hbm.at[chan ^ k], rec.at[k])
        fetch((5, k), (x0, x1, x2, x3)[k], xin.at[k])
        fetch_part(2, k)
        fetch_part(0, k)

    for k in range(4):
        fetch_rows(k)
    fetch_part(1, 0)
    fetch_part(3, 0)
    fetch_part(1, 1)
    fetch_part(3, 1)
    fetch_part(1, 2)
    fetch_part(3, 2)
    fetch_part(1, 3)
    fetch_part(3, 3)
    for n in range(4):
        fetch_part(4, n)
    order = one_hot(
        (512, 512),
        lambda r, k: k == ((r % 256) // 4) * 8 + (r // 256) * 4 + r % 4,
    )
    for k in range(4):
        if k < 2:
            for n in (0,) if k == 0 else (1, 2, 3):
                ready(5, n)
                ready(2, n)
                ready(0, n)
        c = chan ^ k
        mixed = mm(order, rec[k])
        res = xin[k].reshape(512, 512).astype(F32)
        g = gate[c].astype(F32)
        scale = (g[0:1] + g[1:2]) + g[2:3]
        bias = (g[3:4] + g[4:5]) + g[5:6]
        z = scale * res + bias
        hidden = (res + mixed * (0.5 * jnp.tanh(0.5 * z) + 0.5)).astype(BF16)
        hid[c] = hidden
        inner = mm(hidden, w1[c].reshape(512, 512)).astype(BF16)
        for l in range(4):
            mid[l, c] = inner[:, l * 128 : (l + 1) * 128]
    for k in range(4):
        if k % 2 == 0:
            for n in (k, k + 1):
                ready(1, n)
                ready(3, n)
        if k == 2:
            for n in range(4):
                ready(4, n)
        l = chan ^ k
        rows = jnp.concatenate([mid[l, c] for c in range(4)], axis=1)
        for j in range(4):
            e = mm(rows, w2[l, j])
            u = e * (0.7978845608028654 + 0.035677408136300125 * (e * e))
            half = 0.5 * e
            act[:, j * 512 : (j + 1) * 512] = (half + half * jnp.tanh(u)).astype(BF16)
        inner = mm(act[...], w3[l].reshape(2048, 512)).astype(BF16)
        for n in range(4):
            mid2[n, l] = inner[:, n * 128 : (n + 1) * 128]
    stores = []
    for k in range(4):
        n = chan ^ k
        rows = jnp.concatenate([mid2[n, l] for l in range(4)], axis=1)
        t = mm(rows, w4[n].reshape(512, 512))
        out[k] = (hid[n].astype(F32) + t).astype(BF16).reshape(2, 256, 512)
        lanes = pl.ds(pl.multiple_of(n * 512, 512), 512)
        stores.append(pltpu.make_async_copy(out.at[k], o_hbm.at[:, :, lanes], o_sems.at[k]))
        stores[k].start()
    for copy in stores:
        copy.wait()


def mlp(meta, received, xs, own, swapped, near, cross):
    wide = pltpu.VMEM((4, 4, 512, 512), BF16)
    narrow = pltpu.VMEM((4, 4, 128, 512), BF16)
    tall = pltpu.VMEM((4, 4, 512, 128), BF16)
    square = pltpu.VMEM((4, 512, 512), BF16)
    halves = pltpu.VMEM((4, 2, 256, 512), BF16)
    return pl.pallas_call(
        mlp_kernel,
        out_shape=jax.ShapeDtypeStruct((2, 256, 2048), BF16),
        in_specs=[SMEM] + [HBM] * 31,
        out_specs=HBM,
        scratch_shapes=[
            pltpu.VMEM((512, 2048), BF16),
            halves,
            square,
            halves,
            pltpu.VMEM((4, 16, 512), BF16),
            square,
            tall,
            tall,
            narrow,
            wide,
            wide,
            narrow,
            pltpu.SemaphoreType.DMA((80,)),
            pltpu.SemaphoreType.DMA((4,)),
        ],
        compiler_params=params(FULL),
        cost_estimate=pl.CostEstimate(
            flops=11 * 2**30, bytes_accessed=26 * MIB, transcendentals=5 * MIB
        ),
        name="mlp",
    )(meta, received, *xs, *own, *swapped, *near, *cross)


def place(y, z, xl, h, c):
    return (((y % 4) * 8 + z) * 2 + xl) * 4 + h * 2 + c


def pairs(move):
    out = []
    for i in range(256):
        seq, chan = divmod(i, 4)
        y, rest = divmod(seq, 16)
        z, xl = divmod(rest, 2)
        out.append((i, place(*move(y, z, xl, chan // 2, chan % 2))))
    return out


def next_along_x(y, z, xl, h, c):
    return y, z, 1 - xl, 1 - h, c


TO_X = pairs(next_along_x)
TO_CORE = pairs(lambda y, z, xl, h, c: (y, z, xl, h, 1 - c))
TO_CHAN = [
    pairs(lambda y, z, xl, h, c, k=k: (y, z, xl, h ^ (k >> 1), c ^ (k & 1))) for k in range(4)
]


def along_y(step):
    return pairs(lambda y, z, xl, h, c: (y + step, z, xl, h, c))


def on_device(
    inputs, mix_first, mix_second, gate_scale, gate_bias, up_first, up_second, down_first, down_second
):
    bar = lax.optimization_barrier
    chan = lax.axis_index("chan")
    y = lax.axis_index("seq") // 16
    meta = jnp.stack([chan, y]).astype(jnp.int32)
    gate = jnp.stack([gate_scale, gate_bias])
    grouped = inputs.reshape(2, 4, 256, 512)
    move = lambda piece, to: lax.ppermute(piece, BOTH, to)
    swap = lambda piece: lax.ppermute(piece, BOTH, TO_CORE)

    sent = first_mix(grouped, mix_first)
    received = lax.all_to_all(sent, "seq", split_axis=0, concat_axis=0, tiled=True)
    _, meta = bar((sent, meta))
    mine_a, mine_b, mine_far = quarter(meta, gate, up_first, up_second, down_first, down_second)
    _, meta = bar((mine_a, meta))
    near_a, near_b = move(mine_a, TO_X), move(mine_b, TO_X)
    _, mine_far = bar((near_b, mine_far))
    far_b = move(mine_far, TO_X)
    up_a, down_a = move(near_a, along_y(1)), move(near_a, along_y(-1))
    own = pack(meta, gate, up_first, up_second, down_first, down_second)
    spread_second = spread(meta, mix_second)
    received, spread_second, near_a, near_b, far_b, up_a, down_a, own, meta = bar(
        (received, spread_second, near_a, near_b, far_b, up_a, down_a, own, meta)
    )
    swapped, cross_far = [swap(piece) for piece in own], swap(far_b)
    turned = second_mix(received, spread_second)
    turned, swapped, cross_far, near_a, near_b, up_a, down_a, meta = bar(
        (turned, swapped, cross_far, near_a, near_b, up_a, down_a, meta)
    )
    back = lax.all_to_all(turned, ("chan", "seq"), split_axis=0, concat_axis=0, tiled=True)
    xs = []
    for k in range(4):
        part = lax.dynamic_index_in_dim(grouped, meta[0] ^ k, 1, keepdims=False)
        xs.append(move(part, TO_CHAN[k]) if k else part)
    up_b, down_b = move(near_b, along_y(1)), move(near_b, along_y(-1))
    low, high = move(up_a[:LOW], along_y(1)), move(down_a[LOW:], along_y(-1))
    xs, up_b, down_b, low, high, near_a, up_a, down_a = bar(
        (xs, up_b, down_b, low, high, near_a, up_a, down_a)
    )
    near = [near_a, up_a, down_a, low, high, near_b, up_b, down_b, far_b]
    cross = [swap(piece) for piece in near[:8]] + [cross_far]
    return mlp(meta, back.reshape(4, 512, 512), xs, own, swapped, near, cross)


def solution(mesh):
    return jax.shard_map(
        on_device,
        mesh=mesh,
        in_specs=(
            P(None, "seq", "chan"),
            P("seq", None, None),
            P("seq", None, None),
            P("chan"),
            P("chan"),
            P("chan", None, None),
            P("chan", None, None),
            P("chan", None, None),
            P("chan", None, None),
        ),
        out_specs=P(None, ("seq", "chan"), None),
        check_vma=False,
    )
```

```python
import functools

import jax
import jax.numpy as jnp
from jax import lax
from jax.experimental import pallas as pl
from jax.experimental.pallas import tpu as pltpu
from jax.sharding import PartitionSpec as P

BF16 = jnp.bfloat16
F32 = jnp.float32
BOTH = ("seq", "chan")
MIB = 1 << 20
FULL = 58
VMEM = pl.BlockSpec(memory_space=pltpu.VMEM)
HBM = pl.BlockSpec(memory_space=pltpu.HBM)
SMEM = pl.BlockSpec(memory_space=pltpu.SMEM)


def params(mib):
    return pltpu.CompilerParams(vmem_limit_bytes=mib * MIB)


def mm(a, b):
    return jnp.dot(a, b, preferred_element_type=F32)


def mm_nt(a, b):
    return lax.dot_general(a, b, (((1,), (1,)), ((), ())), preferred_element_type=F32)


def iota2(shape, axis):
    return lax.broadcasted_iota(jnp.int32, shape, axis)


def one_hot(shape, pick):
    return jnp.where(pick(iota2(shape, 0), iota2(shape, 1)), 1.0, 0.0).astype(BF16)


def first_kernel(x_hbm, m_hbm, o_ref, acc, x, m, sems):
    copies = []
    for a in range(4):
        copies.append(
            (
                pltpu.make_async_copy(m_hbm.at[a], m.at[a], sems.at[2 * a]),
                pltpu.make_async_copy(x_hbm.at[:, a], x.at[a], sems.at[2 * a + 1]),
            )
        )
    for pair in copies:
        for c in pair:
            c.start()
    for a in range(4):
        for c in copies[a]:
            c.wait()
        for s in range(2):
            acc[:, s * 4 + a, :] = mm(m[a], x[a, s])
    o_ref[...] = acc[...].reshape(64, 32, 512).astype(BF16)


def first_mix(x, m):
    return pl.pallas_call(
        first_kernel,
        out_shape=jax.ShapeDtypeStruct((64, 32, 512), BF16),
        in_specs=[HBM, HBM],
        out_specs=VMEM,
        scratch_shapes=[
            pltpu.VMEM((256, 8, 512), F32),
            pltpu.VMEM((4, 2, 256, 512), BF16),
            pltpu.VMEM((4, 256, 256), BF16),
            pltpu.SemaphoreType.DMA((8,)),
        ],
        compiler_params=params(FULL),
        cost_estimate=pl.CostEstimate(flops=2**29, bytes_accessed=5 * MIB, transcendentals=0),
        name="first_mix",
    )(x, m)


def spread_kernel(meta, m_ref, o_ref):
    rows = one_hot((256, 256), lambda r, x: x == (r % 64) * 4 + r // 64)
    for b in range(4):
        turned = mm(rows, m_ref[b]).astype(BF16)
        for s in range(2):
            slot = (b % 2) * 2 + s
            place = one_hot(
                (256, 1024),
                lambda y, k: k == (y // 4) * 16 + (b % 2) * 8 + s * 4 + y % 4,
            )
            o_ref[b // 2, slot * 256 : (slot + 1) * 256, :] = mm(turned, place).astype(BF16)


def spread(meta, m):
    return pl.pallas_call(
        spread_kernel,
        out_shape=jax.ShapeDtypeStruct((2, 1024, 1024), BF16),
        in_specs=[SMEM, VMEM],
        out_specs=VMEM,
        compiler_params=params(FULL),
        cost_estimate=pl.CostEstimate(flops=2**30, bytes_accessed=5 * MIB, transcendentals=0),
        name="spread",
    )(meta, m)


def second_kernel(r_hbm, m_hbm, o_ref, acc, r, m, sems):
    copies = []
    for p in range(2):
        rows = pl.ds(p * 16, 16)
        copies.append(pltpu.make_async_copy(r_hbm.at[:, rows, :], r.at[p], sems.at[2 * p]))
        copies.append(pltpu.make_async_copy(m_hbm.at[p], m.at[p], sems.at[2 * p + 1]))
    for c in copies:
        c.start()
    for p in range(2):
        copies[2 * p].wait()
        copies[2 * p + 1].wait()
        part = r[p].reshape(1024, 512)
        for slot in range(4):
            b, s = p * 2 + slot // 2, slot % 2
            acc[:, s * 4 + b, :] = mm(m[p, slot * 256 : (slot + 1) * 256, :], part)
    o_ref[...] = acc[...].astype(BF16)


def second_mix(received, m):
    return pl.pallas_call(
        second_kernel,
        out_shape=jax.ShapeDtypeStruct((256, 8, 512), BF16),
        in_specs=[HBM, HBM],
        out_specs=VMEM,
        scratch_shapes=[
            pltpu.VMEM((256, 8, 512), F32),
            pltpu.VMEM((2, 64, 16, 512), BF16),
            pltpu.VMEM((2, 1024, 1024), BF16),
            pltpu.SemaphoreType.DMA((4,)),
        ],
        compiler_params=params(34),
        cost_estimate=pl.CostEstimate(flops=2**31, bytes_accessed=8 * MIB, transcendentals=0),
        name="second_mix",
    )(received, m)


A_ROWS, B_ROWS = 656, 640


def same_rows(n, first):
    return one_hot((n, 512), lambda r, c: c == r + first)


def turned_rows(n, first):
    return one_hot((n, 512), lambda r, m: m == ((r + first) % 128) * 4 + (r + first) // 128)


def gate_rows(g_ref):
    rows = []
    for v in range(2):
        rest = g_ref[v : v + 1, :]
        for _ in range(3):
            part = rest.astype(BF16).astype(F32)
            rows.append(part)
            rest = rest - part
    return jnp.concatenate(rows + [jnp.zeros((10, 512), F32)], axis=0).astype(BF16)


def quarter_kernel(meta, g_ref, w1, w2, w3, w4, a_ref, b_ref, f_ref, v1, v2, v3, v5, v4, sem):
    y = meta[1]
    far = (y + 2) % 4
    near_at, far_at = pl.multiple_of(y * 512, 512), pl.multiple_of(far * 512, 512)
    copies = [
        pltpu.make_async_copy(w1.at[0], v1, sem.at[0]),
        pltpu.make_async_copy(w2.at[0, pl.ds(near_at, 512), :], v2, sem.at[1]),
        pltpu.make_async_copy(w3.at[0, :, pl.ds(near_at, 512)], v3, sem.at[2]),
        pltpu.make_async_copy(w3.at[0, :, pl.ds(far_at, 512)], v5, sem.at[3]),
        pltpu.make_async_copy(w4.at[0], v4, sem.at[4]),
    ]
    for c in copies:
        c.start()
    for c in copies:
        c.wait()
    a_ref[0:128, :] = mm_nt(same_rows(128, y * 128), v1[...]).astype(BF16)
    a_ref[128:640, :] = mm_nt(turned_rows(512, 0), v2[...]).astype(BF16)
    a_ref[640:656, :] = gate_rows(g_ref)
    for at, v, out in ((y, v3, b_ref), (far, v5, f_ref)):
        out[0:512, :] = mm_nt(same_rows(512, 0), v[...]).astype(BF16)
        out[512:640, :] = mm_nt(turned_rows(128, at * 128), v4[...]).astype(BF16)


def quarter(meta, gate, w1, w2, w3, w4):
    b_piece = jax.ShapeDtypeStruct((B_ROWS, 512), BF16)
    return pl.pallas_call(
        quarter_kernel,
        out_shape=(jax.ShapeDtypeStruct((A_ROWS, 512), BF16), b_piece, b_piece),
        in_specs=[SMEM, VMEM] + [HBM] * 4,
        out_specs=(VMEM, VMEM, VMEM),
        scratch_shapes=[pltpu.VMEM((512, 512), BF16)] * 5 + [pltpu.SemaphoreType.DMA((5,))],
        compiler_params=params(FULL),
        cost_estimate=pl.CostEstimate(flops=2**29, bytes_accessed=4 * MIB, transcendentals=0),
        name="quarter",
    )(meta, gate, w1, w2, w3, w4)


def pack_kernel(meta, g_ref, w1, w2, w3, w4, *o_refs):
    same = same_rows(512, 0)
    turn = turned_rows(512, 0)
    first = mm_nt(same, w1[0]).astype(BF16)
    last = mm_nt(turn, w4[0]).astype(BF16)
    for j in range(4):
        wide = slice(j * 512, (j + 1) * 512)
        o_refs[j][0:128, :] = first[j * 128 : (j + 1) * 128]
        o_refs[j][128:640, :] = mm_nt(turn, w2[0, wide, :]).astype(BF16)
        o_refs[j][640:656, :] = gate_rows(g_ref)
        o_refs[j][656:1168, :] = mm_nt(same, w3[0, :, wide]).astype(BF16)
        o_refs[j][1168:1296, :] = last[j * 128 : (j + 1) * 128]


def pack(meta, gate, w1, w2, w3, w4):
    return pl.pallas_call(
        pack_kernel,
        out_shape=(jax.ShapeDtypeStruct((A_ROWS + B_ROWS, 512), BF16),) * 4,
        in_specs=[SMEM] + [VMEM] * 5,
        out_specs=(VMEM,) * 4,
        compiler_params=params(FULL),
        cost_estimate=pl.CostEstimate(flops=2**31, bytes_accessed=10 * MIB, transcendentals=0),
        name="pack",
    )(meta, gate, w1, w2, w3, w4)


LOW = 320
PIECES = (
    (0, 656, 0),
    (0, 656, 3),
    (0, 656, 1),
    (0, LOW, 2),
    (LOW, 656, 2),
    (656, 1296, 0),
    (656, 1296, 3),
    (656, 1296, 1),
    (656, 1296, 2),
)
SPANS = ((0, 128), (128, 640), (640, 656), (656, 1168), (1168, 1296))


def mlp_kernel(
    meta, r_hbm, x0, x1, x2, x3, *refs
):
    own, swapped, refs = refs[:4], refs[4:8], refs[8:]
    pieces, refs = (refs[:9], refs[9:18]), refs[18:]
    o_hbm, act, out, rec, xin, gate, hid, mid, mid2, w1, w2, w3, w4, sems, o_sems = refs
    chan, y = meta[0], meta[1]
    waits = {}
    count = [0]

    def fetch(key, src, dst):
        copy = pltpu.make_async_copy(src, dst, sems.at[count[0]])
        count[0] += 1
        copy.start()
        waits.setdefault(key, []).append(copy)

    def fetch_part(part, k):
        dst = (w1, w2, gate, w3, w4)[part]
        lo, hi = SPANS[part]
        block = chan ^ k
        if k < 2:
            for j in range(1 if part == 2 else 4):
                to = dst.at[block] if part == 2 else dst.at[block, j]
                fetch((part, k), (own, swapped)[k][j].at[lo:hi, :], to)
        else:
            for src, (first, end, offset) in zip(pieces[k - 2], PIECES):
                a, b = max(lo, first), min(hi, end)
                if a >= b or (part == 2 and offset):
                    continue
                to = dst.at[block]
                if part != 2:
                    to = dst.at[block, (y + offset) % 4, a - lo : b - lo, :]
                fetch((part, k), src.at[a - first : b - first, :], to)

    def ready(part, k):
        for copy in waits[(part, k)]:
            copy.wait()

    def fetch_rows(k):
        fetch((5, k), r_hbm.at[chan ^ k], rec.at[k])
        fetch((5, k), (x0, x1, x2, x3)[k], xin.at[k])
        fetch_part(2, k)
        fetch_part(0, k)

    for k in range(4):
        fetch_rows(k)
    fetch_part(1, 0)
    fetch_part(3, 0)
    fetch_part(1, 1)
    fetch_part(3, 1)
    fetch_part(1, 2)
    fetch_part(3, 2)
    fetch_part(1, 3)
    fetch_part(3, 3)
    for n in range(4):
        fetch_part(4, n)
    order = one_hot(
        (512, 512),
        lambda r, k: k == ((r % 256) // 4) * 8 + (r // 256) * 4 + r % 4,
    )
    def first_stage(k, carry):
        @pl.when(k == 1)
        def _():
            for n in (1, 2, 3):
                ready(5, n)
                ready(2, n)
                ready(0, n)

        c = chan ^ k
        mixed = mm(order, rec[k])
        res = xin[k].reshape(512, 512).astype(F32)
        g = gate[c].astype(F32)
        scale = (g[0:1] + g[1:2]) + g[2:3]
        bias = (g[3:4] + g[4:5]) + g[5:6]
        z = scale * res + bias
        hidden = (res + mixed * (0.5 * jnp.tanh(0.5 * z) + 0.5)).astype(BF16)
        hid[c] = hidden
        inner = mm(hidden, w1[c].reshape(512, 512)).astype(BF16)
        for l in range(4):
            mid[l, c] = inner[:, l * 128 : (l + 1) * 128]
        return carry

    def second_stage(k, carry):
        @pl.when(k == 2)
        def _():
            for n in (2, 3):
                ready(1, n)
                ready(3, n)
            for n in range(4):
                ready(4, n)

        l = chan ^ k
        rows = jnp.concatenate([mid[l, c] for c in range(4)], axis=1)
        for j in range(4):
            e = mm(rows, w2[l, j])
            u = e * (0.7978845608028654 + 0.035677408136300125 * (e * e))
            half = 0.5 * e
            act[:, j * 512 : (j + 1) * 512] = (half + half * jnp.tanh(u)).astype(BF16)
        inner = mm(act[...], w3[l].reshape(2048, 512)).astype(BF16)
        for n in range(4):
            mid2[n, l] = inner[:, n * 128 : (n + 1) * 128]
        return carry

    for key in (5, 2, 0):
        ready(key, 0)
    lax.fori_loop(0, 4, first_stage, 0)
    for n in (0, 1):
        ready(1, n)
        ready(3, n)
    lax.fori_loop(0, 4, second_stage, 0)
    stores = []
    for k in range(4):
        n = chan ^ k
        rows = jnp.concatenate([mid2[n, l] for l in range(4)], axis=1)
        t = mm(rows, w4[n].reshape(512, 512))
        out[k] = (hid[n].astype(F32) + t).astype(BF16).reshape(2, 256, 512)
        lanes = pl.ds(pl.multiple_of(n * 512, 512), 512)
        stores.append(pltpu.make_async_copy(out.at[k], o_hbm.at[:, :, lanes], o_sems.at[k]))
        stores[k].start()
    for copy in stores:
        copy.wait()


def mlp(meta, received, xs, own, swapped, near, cross):
    wide = pltpu.VMEM((4, 4, 512, 512), BF16)
    narrow = pltpu.VMEM((4, 4, 128, 512), BF16)
    tall = pltpu.VMEM((4, 4, 512, 128), BF16)
    square = pltpu.VMEM((4, 512, 512), BF16)
    halves = pltpu.VMEM((4, 2, 256, 512), BF16)
    return pl.pallas_call(
        mlp_kernel,
        out_shape=jax.ShapeDtypeStruct((2, 256, 2048), BF16),
        in_specs=[SMEM] + [HBM] * 31,
        out_specs=HBM,
        scratch_shapes=[
            pltpu.VMEM((512, 2048), BF16),
            halves,
            square,
            halves,
            pltpu.VMEM((4, 16, 512), BF16),
            square,
            tall,
            tall,
            narrow,
            wide,
            wide,
            narrow,
            pltpu.SemaphoreType.DMA((80,)),
            pltpu.SemaphoreType.DMA((4,)),
        ],
        compiler_params=params(FULL),
        cost_estimate=pl.CostEstimate(
            flops=11 * 2**30, bytes_accessed=26 * MIB, transcendentals=5 * MIB
        ),
        name="mlp",
    )(meta, received, *xs, *own, *swapped, *near, *cross)


def place(y, z, xl, h, c):
    return (((y % 4) * 8 + z) * 2 + xl) * 4 + h * 2 + c


def pairs(move):
    out = []
    for i in range(256):
        seq, chan = divmod(i, 4)
        y, rest = divmod(seq, 16)
        z, xl = divmod(rest, 2)
        out.append((i, place(*move(y, z, xl, chan // 2, chan % 2))))
    return out


def next_along_x(y, z, xl, h, c):
    return y, z, 1 - xl, 1 - h, c


TO_X = pairs(next_along_x)
TO_CORE = pairs(lambda y, z, xl, h, c: (y, z, xl, h, 1 - c))
TO_CHAN = [
    pairs(lambda y, z, xl, h, c, k=k: (y, z, xl, h ^ (k >> 1), c ^ (k & 1))) for k in range(4)
]


def along_y(step):
    return pairs(lambda y, z, xl, h, c: (y + step, z, xl, h, c))


def on_device(
    inputs, mix_first, mix_second, gate_scale, gate_bias, up_first, up_second, down_first, down_second
):
    bar = lax.optimization_barrier
    chan = lax.axis_index("chan")
    y = lax.axis_index("seq") // 16
    meta = jnp.stack([chan, y]).astype(jnp.int32)
    gate = jnp.stack([gate_scale, gate_bias])
    grouped = inputs.reshape(2, 4, 256, 512)
    move = lambda piece, to: lax.ppermute(piece, BOTH, to)
    swap = lambda piece: lax.ppermute(piece, BOTH, TO_CORE)

    sent = first_mix(grouped, mix_first)
    received = lax.all_to_all(sent, "seq", split_axis=0, concat_axis=0, tiled=True)
    _, meta = bar((sent, meta))
    mine_a, mine_b, mine_far = quarter(meta, gate, up_first, up_second, down_first, down_second)
    _, meta = bar((mine_a, meta))
    near_a, near_b = move(mine_a, TO_X), move(mine_b, TO_X)
    _, mine_far = bar((near_b, mine_far))
    far_b = move(mine_far, TO_X)
    up_a, down_a = move(near_a, along_y(1)), move(near_a, along_y(-1))
    own = pack(meta, gate, up_first, up_second, down_first, down_second)
    spread_second = spread(meta, mix_second)
    received, spread_second, near_a, near_b, far_b, up_a, down_a, own, meta = bar(
        (received, spread_second, near_a, near_b, far_b, up_a, down_a, own, meta)
    )
    swapped, cross_far = [swap(piece) for piece in own], swap(far_b)
    turned = second_mix(received, spread_second)
    turned, swapped, cross_far, near_a, near_b, up_a, down_a, meta = bar(
        (turned, swapped, cross_far, near_a, near_b, up_a, down_a, meta)
    )
    back = lax.all_to_all(turned, ("chan", "seq"), split_axis=0, concat_axis=0, tiled=True)
    xs = []
    for k in range(4):
        part = lax.dynamic_index_in_dim(grouped, meta[0] ^ k, 1, keepdims=False)
        xs.append(move(part, TO_CHAN[k]) if k else part)
    up_b, down_b = move(near_b, along_y(1)), move(near_b, along_y(-1))
    low, high = move(up_a[:LOW], along_y(1)), move(down_a[LOW:], along_y(-1))
    xs, up_b, down_b, low, high, near_a, up_a, down_a = bar(
        (xs, up_b, down_b, low, high, near_a, up_a, down_a)
    )
    near = [near_a, up_a, down_a, low, high, near_b, up_b, down_b, far_b]
    cross = [swap(piece) for piece in near[:8]] + [cross_far]
    return mlp(meta, back.reshape(4, 512, 512), xs, own, swapped, near, cross)


def solution(mesh):
    return jax.shard_map(
        on_device,
        mesh=mesh,
        in_specs=(
            P(None, "seq", "chan"),
            P("seq", None, None),
            P("seq", None, None),
            P("chan"),
            P("chan"),
            P("chan", None, None),
            P("chan", None, None),
            P("chan", None, None),
            P("chan", None, None),
        ),
        out_specs=P(None, ("seq", "chan"), None),
        check_vma=False,
    )
```

```python
import functools

import jax
import jax.numpy as jnp
from jax import lax
from jax.experimental import pallas as pl
from jax.experimental.pallas import tpu as pltpu
from jax.sharding import PartitionSpec as P

BF16 = jnp.bfloat16
F32 = jnp.float32
BOTH = ("seq", "chan")
MIB = 1 << 20
FULL = 58
VMEM = pl.BlockSpec(memory_space=pltpu.VMEM)
HBM = pl.BlockSpec(memory_space=pltpu.HBM)
SMEM = pl.BlockSpec(memory_space=pltpu.SMEM)


def params(mib):
    return pltpu.CompilerParams(vmem_limit_bytes=mib * MIB)


def mm(a, b):
    return jnp.dot(a, b, preferred_element_type=F32)


def mm_nt(a, b):
    return lax.dot_general(a, b, (((1,), (1,)), ((), ())), preferred_element_type=F32)


def iota2(shape, axis):
    return lax.broadcasted_iota(jnp.int32, shape, axis)


def one_hot(shape, pick):
    return jnp.where(pick(iota2(shape, 0), iota2(shape, 1)), 1.0, 0.0).astype(BF16)


def first_kernel(x_hbm, m_hbm, o_ref, acc, x, m, sems):
    copies = []
    for a in range(4):
        copies.append(
            (
                pltpu.make_async_copy(m_hbm.at[a], m.at[a], sems.at[2 * a]),
                pltpu.make_async_copy(x_hbm.at[:, a], x.at[a], sems.at[2 * a + 1]),
            )
        )
    for pair in copies:
        for c in pair:
            c.start()
    for a in range(4):
        for c in copies[a]:
            c.wait()
        for s in range(2):
            acc[:, s * 4 + a, :] = mm(m[a], x[a, s])
    o_ref[...] = acc[...].reshape(64, 32, 512).astype(BF16)


def first_mix(x, m):
    return pl.pallas_call(
        first_kernel,
        out_shape=jax.ShapeDtypeStruct((64, 32, 512), BF16),
        in_specs=[HBM, HBM],
        out_specs=VMEM,
        scratch_shapes=[
            pltpu.VMEM((256, 8, 512), F32),
            pltpu.VMEM((4, 2, 256, 512), BF16),
            pltpu.VMEM((4, 256, 256), BF16),
            pltpu.SemaphoreType.DMA((8,)),
        ],
        compiler_params=params(FULL),
        cost_estimate=pl.CostEstimate(flops=2**29, bytes_accessed=5 * MIB, transcendentals=0),
        name="first_mix",
    )(x, m)


def spread_kernel(meta, m_ref, o_ref):
    rows = one_hot((256, 256), lambda r, x: x == (r % 64) * 4 + r // 64)
    for b in range(4):
        turned = mm(rows, m_ref[b]).astype(BF16)
        for s in range(2):
            slot = (b % 2) * 2 + s
            place = one_hot(
                (256, 1024),
                lambda y, k: k == (y // 4) * 16 + (b % 2) * 8 + s * 4 + y % 4,
            )
            o_ref[b // 2, slot * 256 : (slot + 1) * 256, :] = mm(turned, place).astype(BF16)


def spread(meta, m):
    return pl.pallas_call(
        spread_kernel,
        out_shape=jax.ShapeDtypeStruct((2, 1024, 1024), BF16),
        in_specs=[SMEM, VMEM],
        out_specs=VMEM,
        compiler_params=params(FULL),
        cost_estimate=pl.CostEstimate(flops=2**30, bytes_accessed=5 * MIB, transcendentals=0),
        name="spread",
    )(meta, m)


def second_kernel(r_hbm, m_hbm, o_ref, acc, r, m, sems):
    copies = []
    for p in range(2):
        rows = pl.ds(p * 16, 16)
        copies.append(pltpu.make_async_copy(r_hbm.at[:, rows, :], r.at[p], sems.at[2 * p]))
        copies.append(pltpu.make_async_copy(m_hbm.at[p], m.at[p], sems.at[2 * p + 1]))
    for c in copies:
        c.start()
    for p in range(2):
        copies[2 * p].wait()
        copies[2 * p + 1].wait()
        part = r[p].reshape(1024, 512)
        for slot in range(4):
            b, s = p * 2 + slot // 2, slot % 2
            acc[:, s * 4 + b, :] = mm(m[p, slot * 256 : (slot + 1) * 256, :], part)
    o_ref[...] = acc[...].astype(BF16)


def second_mix(received, m):
    return pl.pallas_call(
        second_kernel,
        out_shape=jax.ShapeDtypeStruct((256, 8, 512), BF16),
        in_specs=[HBM, HBM],
        out_specs=VMEM,
        scratch_shapes=[
            pltpu.VMEM((256, 8, 512), F32),
            pltpu.VMEM((2, 64, 16, 512), BF16),
            pltpu.VMEM((2, 1024, 1024), BF16),
            pltpu.SemaphoreType.DMA((4,)),
        ],
        compiler_params=params(34),
        cost_estimate=pl.CostEstimate(flops=2**31, bytes_accessed=8 * MIB, transcendentals=0),
        name="second_mix",
    )(received, m)


A_ROWS, B_ROWS = 656, 640


def same_rows(n, first):
    return one_hot((n, 512), lambda r, c: c == r + first)


def turned_rows(n, first):
    return one_hot((n, 512), lambda r, m: m == ((r + first) % 128) * 4 + (r + first) // 128)


def gate_rows(g_ref):
    rows = []
    for v in range(2):
        rest = g_ref[v : v + 1, :]
        for _ in range(3):
            part = rest.astype(BF16).astype(F32)
            rows.append(part)
            rest = rest - part
    return jnp.concatenate(rows + [jnp.zeros((10, 512), F32)], axis=0).astype(BF16)


def quarter_a_kernel(meta, g_ref, w1, w2, a_ref, v1, v2, sem):
    y = meta[1]
    at = pl.multiple_of(y * 512, 512)
    copies = [
        pltpu.make_async_copy(w1.at[0], v1, sem.at[0]),
        pltpu.make_async_copy(w2.at[0, pl.ds(at, 512), :], v2, sem.at[1]),
    ]
    for c in copies:
        c.start()
    for c in copies:
        c.wait()
    a_ref[0:128, :] = mm_nt(same_rows(128, y * 128), v1[...]).astype(BF16)
    a_ref[128:640, :] = mm_nt(turned_rows(512, 0), v2[...]).astype(BF16)
    a_ref[640:656, :] = gate_rows(g_ref)


def quarter_a(meta, gate, w1, w2):
    return pl.pallas_call(
        quarter_a_kernel,
        out_shape=jax.ShapeDtypeStruct((A_ROWS, 512), BF16),
        in_specs=[SMEM, VMEM, HBM, HBM],
        out_specs=VMEM,
        scratch_shapes=[pltpu.VMEM((512, 512), BF16)] * 2 + [pltpu.SemaphoreType.DMA((2,))],
        compiler_params=params(FULL),
        cost_estimate=pl.CostEstimate(flops=2**28, bytes_accessed=2 * MIB, transcendentals=0),
        name="quarter_a",
    )(meta, gate, w1, w2)


def quarter_b_kernel(meta, w3, w4, b_ref, f_ref, v3, v5, v4, sem):
    y = meta[1]
    far = (y + 2) % 4
    near_at, far_at = pl.multiple_of(y * 512, 512), pl.multiple_of(far * 512, 512)
    copies = [
        pltpu.make_async_copy(w3.at[0, :, pl.ds(near_at, 512)], v3, sem.at[0]),
        pltpu.make_async_copy(w3.at[0, :, pl.ds(far_at, 512)], v5, sem.at[1]),
        pltpu.make_async_copy(w4.at[0], v4, sem.at[2]),
    ]
    for c in copies:
        c.start()
    for c in copies:
        c.wait()
    for at, v, out in ((y, v3, b_ref), (far, v5, f_ref)):
        out[0:512, :] = mm_nt(same_rows(512, 0), v[...]).astype(BF16)
        out[512:640, :] = mm_nt(turned_rows(128, at * 128), v4[...]).astype(BF16)


def quarter_b(meta, w3, w4):
    piece = jax.ShapeDtypeStruct((B_ROWS, 512), BF16)
    return pl.pallas_call(
        quarter_b_kernel,
        out_shape=(piece, piece),
        in_specs=[SMEM, HBM, HBM],
        out_specs=(VMEM, VMEM),
        scratch_shapes=[pltpu.VMEM((512, 512), BF16)] * 3 + [pltpu.SemaphoreType.DMA((3,))],
        compiler_params=params(FULL),
        cost_estimate=pl.CostEstimate(flops=2**28, bytes_accessed=3 * MIB, transcendentals=0),
        name="quarter_b",
    )(meta, w3, w4)


def pack_kernel(meta, g_ref, w1, w2, w3, w4, *o_refs):
    same = same_rows(512, 0)
    turn = turned_rows(512, 0)
    first = mm_nt(same, w1[0]).astype(BF16)
    last = mm_nt(turn, w4[0]).astype(BF16)
    for j in range(4):
        wide = slice(j * 512, (j + 1) * 512)
        o_refs[j][0:128, :] = first[j * 128 : (j + 1) * 128]
        o_refs[j][128:640, :] = mm_nt(turn, w2[0, wide, :]).astype(BF16)
        o_refs[j][640:656, :] = gate_rows(g_ref)
        o_refs[j][656:1168, :] = mm_nt(same, w3[0, :, wide]).astype(BF16)
        o_refs[j][1168:1296, :] = last[j * 128 : (j + 1) * 128]


def pack(meta, gate, w1, w2, w3, w4):
    return pl.pallas_call(
        pack_kernel,
        out_shape=(jax.ShapeDtypeStruct((A_ROWS + B_ROWS, 512), BF16),) * 4,
        in_specs=[SMEM] + [VMEM] * 5,
        out_specs=(VMEM,) * 4,
        compiler_params=params(FULL),
        cost_estimate=pl.CostEstimate(flops=2**31, bytes_accessed=10 * MIB, transcendentals=0),
        name="pack",
    )(meta, gate, w1, w2, w3, w4)


LOW = 320
PIECES = (
    (0, 656, 0),
    (0, 656, 3),
    (0, 656, 1),
    (0, LOW, 2),
    (LOW, 656, 2),
    (656, 1296, 0),
    (656, 1296, 3),
    (656, 1296, 1),
    (656, 1296, 2),
)
SPANS = ((0, 128), (128, 640), (640, 656), (656, 1168), (1168, 1296))


def mlp_kernel(
    meta, r_hbm, x0, x1, x2, x3, *refs
):
    own, swapped, refs = refs[:4], refs[4:8], refs[8:]
    pieces, refs = (refs[:9], refs[9:18]), refs[18:]
    o_hbm, act, out, rec, xin, gate, hid, mid, mid2, w1, w2, w3, w4, sems, o_sems = refs
    chan, y = meta[0], meta[1]
    waits = {}
    count = [0]

    def fetch(key, src, dst):
        copy = pltpu.make_async_copy(src, dst, sems.at[count[0]])
        count[0] += 1
        copy.start()
        waits.setdefault(key, []).append(copy)

    def fetch_part(part, k):
        dst = (w1, w2, gate, w3, w4)[part]
        lo, hi = SPANS[part]
        block = chan ^ k
        if k < 2:
            for j in range(1 if part == 2 else 4):
                to = dst.at[block] if part == 2 else dst.at[block, j]
                fetch((part, k), (own, swapped)[k][j].at[lo:hi, :], to)
        else:
            for src, (first, end, offset) in zip(pieces[k - 2], PIECES):
                a, b = max(lo, first), min(hi, end)
                if a >= b or (part == 2 and offset):
                    continue
                to = dst.at[block]
                if part != 2:
                    to = dst.at[block, (y + offset) % 4, a - lo : b - lo, :]
                fetch((part, k), src.at[a - first : b - first, :], to)

    def ready(part, k):
        for copy in waits[(part, k)]:
            copy.wait()

    def fetch_rows(k):
        fetch((5, k), r_hbm.at[chan ^ k], rec.at[k])
        fetch((5, k), (x0, x1, x2, x3)[k], xin.at[k])
        fetch_part(2, k)
        fetch_part(0, k)

    for k in range(4):
        fetch_rows(k)
    fetch_part(1, 0)
    fetch_part(3, 0)
    fetch_part(1, 1)
    fetch_part(3, 1)
    fetch_part(1, 2)
    fetch_part(3, 2)
    fetch_part(1, 3)
    fetch_part(3, 3)
    for n in range(4):
        fetch_part(4, n)
    order = one_hot(
        (512, 512),
        lambda r, k: k == ((r % 256) // 4) * 8 + (r // 256) * 4 + r % 4,
    )
    def first_stage(k, carry):
        @pl.when(k == 1)
        def _():
            for n in (1, 2, 3):
                ready(5, n)
                ready(2, n)
                ready(0, n)

        c = chan ^ k
        mixed = mm(order, rec[k])
        res = xin[k].reshape(512, 512).astype(F32)
        g = gate[c].astype(F32)
        scale = (g[0:1] + g[1:2]) + g[2:3]
        bias = (g[3:4] + g[4:5]) + g[5:6]
        z = scale * res + bias
        hidden = (res + mixed * (0.5 * jnp.tanh(0.5 * z) + 0.5)).astype(BF16)
        hid[c] = hidden
        inner = mm(hidden, w1[c].reshape(512, 512)).astype(BF16)
        for l in range(4):
            mid[l, c] = inner[:, l * 128 : (l + 1) * 128]
        return carry

    def second_stage(k, carry):
        @pl.when(k == 2)
        def _():
            for n in (2, 3):
                ready(1, n)
                ready(3, n)
            for n in range(4):
                ready(4, n)

        l = chan ^ k
        rows = jnp.concatenate([mid[l, c] for c in range(4)], axis=1)
        for j in range(4):
            e = mm(rows, w2[l, j])
            u = e * (0.7978845608028654 + 0.035677408136300125 * (e * e))
            half = 0.5 * e
            act[:, j * 512 : (j + 1) * 512] = (half + half * jnp.tanh(u)).astype(BF16)
        inner = mm(act[...], w3[l].reshape(2048, 512)).astype(BF16)
        for n in range(4):
            mid2[n, l] = inner[:, n * 128 : (n + 1) * 128]
        return carry

    for key in (5, 2, 0):
        ready(key, 0)
    lax.fori_loop(0, 4, first_stage, 0)
    for n in (0, 1):
        ready(1, n)
        ready(3, n)
    lax.fori_loop(0, 4, second_stage, 0)
    stores = []
    for k in range(4):
        n = chan ^ k
        rows = jnp.concatenate([mid2[n, l] for l in range(4)], axis=1)
        t = mm(rows, w4[n].reshape(512, 512))
        out[k] = (hid[n].astype(F32) + t).astype(BF16).reshape(2, 256, 512)
        lanes = pl.ds(pl.multiple_of(n * 512, 512), 512)
        stores.append(pltpu.make_async_copy(out.at[k], o_hbm.at[:, :, lanes], o_sems.at[k]))
        stores[k].start()
    for copy in stores:
        copy.wait()


def mlp(meta, received, xs, own, swapped, near, cross):
    wide = pltpu.VMEM((4, 4, 512, 512), BF16)
    narrow = pltpu.VMEM((4, 4, 128, 512), BF16)
    tall = pltpu.VMEM((4, 4, 512, 128), BF16)
    square = pltpu.VMEM((4, 512, 512), BF16)
    halves = pltpu.VMEM((4, 2, 256, 512), BF16)
    return pl.pallas_call(
        mlp_kernel,
        out_shape=jax.ShapeDtypeStruct((2, 256, 2048), BF16),
        in_specs=[SMEM] + [HBM] * 31,
        out_specs=HBM,
        scratch_shapes=[
            pltpu.VMEM((512, 2048), BF16),
            halves,
            square,
            halves,
            pltpu.VMEM((4, 16, 512), BF16),
            square,
            tall,
            tall,
            narrow,
            wide,
            wide,
            narrow,
            pltpu.SemaphoreType.DMA((80,)),
            pltpu.SemaphoreType.DMA((4,)),
        ],
        compiler_params=params(FULL),
        cost_estimate=pl.CostEstimate(
            flops=11 * 2**30, bytes_accessed=26 * MIB, transcendentals=5 * MIB
        ),
        name="mlp",
    )(meta, received, *xs, *own, *swapped, *near, *cross)


def place(y, z, xl, h, c):
    return (((y % 4) * 8 + z) * 2 + xl) * 4 + h * 2 + c


def pairs(move):
    out = []
    for i in range(256):
        seq, chan = divmod(i, 4)
        y, rest = divmod(seq, 16)
        z, xl = divmod(rest, 2)
        out.append((i, place(*move(y, z, xl, chan // 2, chan % 2))))
    return out


def next_along_x(y, z, xl, h, c):
    return y, z, 1 - xl, 1 - h, c


TO_X = pairs(next_along_x)
TO_CORE = pairs(lambda y, z, xl, h, c: (y, z, xl, h, 1 - c))
TO_CHAN = [
    pairs(lambda y, z, xl, h, c, k=k: (y, z, xl, h ^ (k >> 1), c ^ (k & 1))) for k in range(4)
]


def along_y(step):
    return pairs(lambda y, z, xl, h, c: (y + step, z, xl, h, c))


def on_device(
    inputs, mix_first, mix_second, gate_scale, gate_bias, up_first, up_second, down_first, down_second
):
    bar = lax.optimization_barrier
    chan = lax.axis_index("chan")
    y = lax.axis_index("seq") // 16
    meta = jnp.stack([chan, y]).astype(jnp.int32)
    gate = jnp.stack([gate_scale, gate_bias])
    grouped = inputs.reshape(2, 4, 256, 512)
    move = lambda piece, to: lax.ppermute(piece, BOTH, to)
    swap = lambda piece: lax.ppermute(piece, BOTH, TO_CORE)

    sent = first_mix(grouped, mix_first)
    received = lax.all_to_all(sent, "seq", split_axis=0, concat_axis=0, tiled=True)
    _, meta = bar((sent, meta))
    mine_a = quarter_a(meta, gate, up_first, up_second)
    _, meta = bar((mine_a, meta))
    mine_b, mine_far = quarter_b(meta, down_first, down_second)
    near_a, near_b = move(mine_a, TO_X), move(mine_b, TO_X)
    _, mine_far = bar((near_b, mine_far))
    far_b = move(mine_far, TO_X)
    up_a, down_a = move(near_a, along_y(1)), move(near_a, along_y(-1))
    own = pack(meta, gate, up_first, up_second, down_first, down_second)
    spread_second = spread(meta, mix_second)
    received, spread_second, near_a, near_b, far_b, up_a, down_a, own, meta = bar(
        (received, spread_second, near_a, near_b, far_b, up_a, down_a, own, meta)
    )
    swapped, cross_far = [swap(piece) for piece in own], swap(far_b)
    turned = second_mix(received, spread_second)
    turned, swapped, cross_far, near_a, near_b, up_a, down_a, meta = bar(
        (turned, swapped, cross_far, near_a, near_b, up_a, down_a, meta)
    )
    back = lax.all_to_all(turned, ("chan", "seq"), split_axis=0, concat_axis=0, tiled=True)
    xs = []
    for k in range(4):
        part = lax.dynamic_index_in_dim(grouped, meta[0] ^ k, 1, keepdims=False)
        xs.append(move(part, TO_CHAN[k]) if k else part)
    up_b, down_b = move(near_b, along_y(1)), move(near_b, along_y(-1))
    low, high = move(up_a[:LOW], along_y(1)), move(down_a[LOW:], along_y(-1))
    xs, up_b, down_b, low, high, near_a, up_a, down_a = bar(
        (xs, up_b, down_b, low, high, near_a, up_a, down_a)
    )
    near = [near_a, up_a, down_a, low, high, near_b, up_b, down_b, far_b]
    cross = [swap(piece) for piece in near[:8]] + [cross_far]
    return mlp(meta, back.reshape(4, 512, 512), xs, own, swapped, near, cross)


def solution(mesh):
    return jax.shard_map(
        on_device,
        mesh=mesh,
        in_specs=(
            P(None, "seq", "chan"),
            P("seq", None, None),
            P("seq", None, None),
            P("chan"),
            P("chan"),
            P("chan", None, None),
            P("chan", None, None),
            P("chan", None, None),
            P("chan", None, None),
        ),
        out_specs=P(None, ("seq", "chan"), None),
        check_vma=False,
    )
```
